256 devices in a mesh: dp: 32 (over y, z), tensor: 4 (over x), section: 2 (over core).
Axes of the slice: x: 4, y: 4, z: 8, core: 2. Of those that a mesh axis runs over, the one named last changes fastest.
Arguments:
- query_heads: bfloat16 [32768, 4, 8, 128], P('dp', 'tensor', 'section'), may hold values from -5 to 5, as said below
- key_heads: bfloat16 [32768, 4, 128], P('dp', 'tensor'), may hold values from -5 to 5, as said below
- value_heads: bfloat16 [32768, 4, 128], P('dp', 'tensor'), may hold values from -6 to 6
- attend_grad: bfloat16 [32768, 4, 8, 128], P('dp', 'tensor', 'section'), may hold values from -6 to 6
- doc_ids: int32 [32768], P('dp'), may hold values from 0 to 31, as said below
- cell_plan: int32 [512], P('dp'), may hold values from -1 to 31, as said below
Outputs:
- query_grad: bfloat16 [32768, 4, 8, 128], P('dp', 'tensor', 'section')
- key_grad: bfloat16 [32768, 4, 128], P('dp', 'tensor')
- value_grad: bfloat16 [32768, 4, 128], P('dp', 'tensor')
The draws below stay inside these ranges and needn't reach their ends.
Inputs may be any that keep to these rules, and one draw needn't show every extreme that they name: `doc_ids`: never falling along a replica. In every cell of 64 tokens it changes exactly once, at the cell's fifth token or later; the cell's first token differs from the last token of the cell before it. `cell_plan`: in a quarter of the replicas the first 8 cells stay (-1) and the others are sent; in the other replicas every cell is sent. A sent cell has the value dest + slot: dest is the replica that receives it, which never keeps cells, and slot tells apart the cells of one replica that go to one replica. Some replica sends exactly 1 cell to one replica. Every replica receives at most 19 cells, and some receive exactly 19. `query_heads`: real values. `key_heads`: real values.
All inputs are finite; a program needn't handle non-finite values.
Results may differ from the reference program's by a relative error of at most 0.025.
Values may be sent and summed in bfloat16 or wider, within the bound.
A program may use at most 64 MiB of HBM per device.

```python
import jax
import jax.numpy as jnp
from jax import lax

KVH = 4
GROUP = 8
HD = 128
CELLS = 16
LONG = 8
CELL = 64
T_REP = 1024
TOKENS = 32768
CAP = 1
SLOTS = 32
RECV = 19
N_DP = 32


def draw_query_heads(key, part):
    key = jax.random.fold_in(key, 1)
    return jnp.clip(jax.random.normal(key, (TOKENS, KVH, GROUP, HD)), -5.0, 5.0).astype(jnp.bfloat16)


def draw_key_heads(key, part):
    key = jax.random.fold_in(key, 2)
    return jnp.clip(jax.random.normal(key, (TOKENS, KVH, HD)), -5.0, 5.0).astype(jnp.bfloat16)


def draw_doc_ids(key, part):
    key = jax.random.fold_in(key, 3)
    score = jax.random.randint(key, (N_DP, CELLS, CELL - 4), 0, 1 << 20)
    score = score * CELL + jnp.arange(CELL - 4, dtype=jnp.int32)
    rank_pos = jnp.argsort(jnp.argsort(score, axis=-1), axis=-1)
    inner_start = (rank_pos < 1).astype(jnp.int32)
    head_flag = jnp.broadcast_to(jnp.array([1, 0, 0, 0], dtype=jnp.int32), (N_DP, CELLS, 4))
    start_flag = jnp.concatenate([head_flag, inner_start], axis=-1).reshape(N_DP, T_REP)
    doc_number = jnp.cumsum(start_flag, axis=1) - 1
    return doc_number.reshape(-1).astype(jnp.int32)


def draw_cell_plan(key, part):
    key = jax.random.fold_in(key, 4)
    order_key, source_key = jax.random.split(key)
    heavy_count = N_DP // 4
    period = N_DP - heavy_count
    counting = jnp.arange(N_DP, dtype=jnp.int32)
    rep_order = jax.random.permutation(order_key, N_DP).astype(jnp.int32)
    rep_rank = jnp.zeros((N_DP,), jnp.int32).at[rep_order].set(counting)
    heavy = rep_rank < heavy_count
    source_order = jax.random.permutation(source_key, N_DP).astype(jnp.int32)
    source_rank = jnp.zeros((N_DP,), jnp.int32).at[source_order].set(counting)
    moved = jnp.where(heavy, CELLS - LONG, CELLS)
    before = source_rank[None, :] < source_rank[:, None]
    run_start = jnp.sum(jnp.where(before, moved[None, :], 0), axis=1)
    cell_index = jnp.arange(CELLS, dtype=jnp.int32)
    run_pos = jnp.where(heavy[:, None], cell_index[None, :] - LONG, cell_index[None, :])
    keep_cell = heavy[:, None] & (cell_index[None, :] < LONG)
    seq_index = run_start[:, None] + jnp.maximum(run_pos, 0)
    light_list = rep_order[heavy_count:]
    dest_rep = light_list[seq_index % period]
    slot_num = jnp.maximum(run_pos, 0) // period
    send_code = dest_rep * CAP + slot_num
    return jnp.where(keep_cell, -1, send_code).reshape(-1).astype(jnp.int32)


def levels(key, shape, shards, low, largest):
    def one(dim, parts):
        heights = jax.random.uniform(jax.random.fold_in(jax.random.fold_in(key, 6), dim), (parts,), jnp.float32, low / len(shards), largest / len(shards))
        return jnp.repeat(jnp.exp(heights), shape[dim] // parts).reshape((-1,) + (1,) * (len(shape) - dim - 1))

    gain = one(*shards[0])
    for cut in shards[1:]:
        gain = gain * one(*cut)
    return gain


def scatter_about(rng, shape, scale, limit, cuts=(), held_as=jnp.bfloat16):
    drawn = scale * jax.random.normal(rng, shape, jnp.float32)
    if cuts:
        drawn = drawn * levels(rng, shape, cuts, -0.22, 0.18)
    return jnp.clip(drawn, -limit, limit).astype(held_as)


def setup_inputs(seed: int = 0) -> dict:
    arg_keys = jax.random.split(jax.random.key(seed), 7)
    return {
        "query_heads": draw_query_heads(jax.random.fold_in(arg_keys[6], 71), 0),
        "key_heads": draw_key_heads(jax.random.fold_in(arg_keys[6], 71), 0),
        "value_heads": scatter_about(arg_keys[2], (TOKENS, KVH, HD), 1.0, 6.0, ((0, 32), (1, 4))),
        "attend_grad": scatter_about(arg_keys[3], (TOKENS, KVH, GROUP, HD), 1.0, 6.0, ((0, 32), (1, 4), (2, 2))),
        "doc_ids": draw_doc_ids(jax.random.fold_in(arg_keys[6], 71), 0),
        "cell_plan": draw_cell_plan(jax.random.fold_in(arg_keys[6], 71), 0),
    }


def attention_grads(query_rows, key_rows, value_rows, grad_rows, query_labels, key_labels, query_pos, key_pos):
    inv_root = HD ** -0.5
    query_f = query_rows.astype(jnp.float32)
    key_f = key_rows.astype(jnp.float32)
    value_f = value_rows.astype(jnp.float32)
    grad_f = grad_rows.astype(jnp.float32)
    scores = jnp.einsum("lkgd,mkd->kglm", query_f, key_f) * inv_root
    allowed = (query_labels[:, None] == key_labels[None, :]) & (key_pos[None, :] <= query_pos[:, None])
    scores = jnp.where(allowed, scores, -jnp.inf)
    row_max = jnp.max(scores, axis=-1, keepdims=True)
    unnorm = jnp.exp(scores - row_max)
    prob_rows = unnorm / jnp.sum(unnorm, axis=-1, keepdims=True)
    weight_f = lax.optimization_barrier(prob_rows.astype(jnp.bfloat16)).astype(jnp.float32)
    attended = jnp.einsum("kglm,mkd->lkgd", weight_f, value_f).astype(jnp.bfloat16)
    attended_f = lax.optimization_barrier(attended).astype(jnp.float32)
    row_delta = jnp.transpose(jnp.sum(grad_f * attended_f, axis=-1), (1, 2, 0))
    prob_grad = jnp.einsum("lkgd,mkd->kglm", grad_f, value_f)
    dscore = lax.optimization_barrier((prob_rows * (prob_grad - row_delta[..., None])).astype(jnp.bfloat16)).astype(jnp.float32)
    query_grad = (jnp.einsum("kglm,mkd->lkgd", dscore, key_f) * inv_root).astype(jnp.bfloat16)
    key_grad = jnp.einsum("kglm,lkgd->mkd", dscore, query_f) * inv_root
    value_grad = jnp.einsum("kglm,lkgd->mkd", weight_f, grad_f)
    return query_grad, key_grad, value_grad


def earlier(source, fill):
    first = jnp.full((1,) + source.shape[1:], fill, source.dtype)
    return jnp.concatenate([first, source[:-1]], axis=0)


def window_grads(inputs):
    query_cells, key_cells, value_cells, grad_cells, label_cells = inputs
    window_keys = jnp.concatenate([earlier(key_cells, 0), key_cells], axis=1)
    window_values = jnp.concatenate([earlier(value_cells, 0), value_cells], axis=1)
    window_labels = jnp.concatenate([earlier(label_cells, -3), label_cells], axis=1)
    position = jnp.arange(2 * CELL, dtype=jnp.int32)

    def one_cell(cell_inputs):
        query_c, key_c, value_c, grad_c, label_q, label_k = cell_inputs
        return attention_grads(query_c, key_c, value_c, grad_c, label_q, label_k, position[CELL:], position)

    query_grad, key_part, value_part = lax.map(one_cell, (query_cells, window_keys, window_values, grad_cells, label_cells, window_labels))

    def fold(part):
        later = jnp.concatenate([part[1:, :CELL], jnp.zeros_like(part[:1, :CELL])], axis=0)
        return part[:, CELL:] + later

    return query_grad, fold(key_part).astype(jnp.bfloat16), fold(value_part).astype(jnp.bfloat16)


def long_grads(inputs):
    query_rows, key_rows, value_rows, grad_rows = inputs
    length = LONG * CELL
    labels = jnp.zeros((length,), jnp.int32)
    position = jnp.arange(length, dtype=jnp.int32)
    query_grad, key_grad, value_grad = attention_grads(query_rows, key_rows, value_rows, grad_rows, labels, labels, position, position)
    return query_grad, key_grad.astype(jnp.bfloat16), value_grad.astype(jnp.bfloat16)


def reference(query_heads, key_heads, value_heads, attend_grad, doc_ids, cell_plan):
    n_cells = N_DP * CELLS
    query_c = query_heads.reshape(n_cells, CELL, KVH, GROUP, HD)
    key_c = key_heads.reshape(n_cells, CELL, KVH, HD)
    value_c = value_heads.reshape(n_cells, CELL, KVH, HD)
    grad_c = attend_grad.reshape(n_cells, CELL, KVH, GROUP, HD)
    doc_c = doc_ids.reshape(n_cells, CELL)
    flags = jnp.concatenate([jnp.zeros((n_cells, 1), jnp.int32), (doc_c[:, 1:] != doc_c[:, :-1]).astype(jnp.int32)], axis=1)
    counting = jnp.arange(n_cells, dtype=jnp.int32)
    sent = cell_plan >= 0
    dest = jnp.where(sent, cell_plan // CAP, N_DP).astype(jnp.int32)
    slot = jnp.where(sent, cell_plan % CAP, 0).astype(jnp.int32)
    source = counting // CELLS
    sort_key = jnp.where(sent, dest * SLOTS + source * CAP + slot, N_DP * SLOTS + counting).astype(jnp.int32)
    order = jnp.argsort(sort_key).astype(jnp.int32)
    dest_sorted = dest[order]
    first = jnp.sum((dest_sorted[None, :] < jnp.arange(N_DP, dtype=jnp.int32)[:, None]).astype(jnp.int32), axis=1)
    rank = counting - first[jnp.minimum(dest_sorted, N_DP - 1)]
    table = jnp.full((N_DP, RECV), n_cells, jnp.int32).at[dest_sorted, rank].set(order, mode="drop")
    valid = table < n_cells
    safe = jnp.minimum(table, n_cells - 1)
    stream_query = jnp.where(valid[:, :, None, None, None, None], query_c[safe], 0).astype(jnp.bfloat16)
    stream_key = jnp.where(valid[:, :, None, None, None], key_c[safe], 0).astype(jnp.bfloat16)
    stream_value = jnp.where(valid[:, :, None, None, None], value_c[safe], 0).astype(jnp.bfloat16)
    stream_grad = jnp.where(valid[:, :, None, None, None, None], grad_c[safe], 0).astype(jnp.bfloat16)
    stream_flags = jnp.where(valid[:, :, None], flags[safe], 0)
    stream_labels = (jnp.cumsum(stream_flags.reshape(N_DP, RECV * CELL), axis=1) - 1).reshape(N_DP, RECV, CELL)
    stream_labels = jnp.where(valid[:, :, None], stream_labels + 1, -2).astype(jnp.int32)
    stream_res = lax.map(window_grads, (stream_query, stream_key, stream_value, stream_grad, stream_labels))
    long_len = LONG * CELL
    long_res = lax.map(long_grads, (query_heads.reshape(N_DP, T_REP, KVH, GROUP, HD)[:, :long_len], key_heads.reshape(N_DP, T_REP, KVH, HD)[:, :long_len], value_heads.reshape(N_DP, T_REP, KVH, HD)[:, :long_len], attend_grad.reshape(N_DP, T_REP, KVH, GROUP, HD)[:, :long_len]))
    keep = (cell_plan < 0).reshape(N_DP, CELLS)
    flat_table = table.reshape(-1)
    outputs = []
    shapes = [(KVH, GROUP, HD), (KVH, HD), (KVH, HD)]
    for which in range(3):
        tail = shapes[which]
        cells_out = jnp.zeros((n_cells, CELL) + tail, jnp.bfloat16)
        cells_out = cells_out.at[flat_table].set(stream_res[which].reshape((N_DP * RECV, CELL) + tail), mode="drop")
        cells_out = cells_out.reshape((N_DP, CELLS, CELL) + tail)
        long_cells = long_res[which].reshape((N_DP, LONG, CELL) + tail)
        mask = keep[:, :LONG].reshape((N_DP, LONG) + (1,) * (len(tail) + 1))
        head = jnp.where(mask, long_cells, cells_out[:, :LONG])
        cells_out = jnp.concatenate([head, cells_out[:, LONG:]], axis=1)
        outputs.append(cells_out.reshape((TOKENS,) + tail))
    return outputs[0], outputs[1], outputs[2]
```

```python
import functools

import jax
import jax.numpy as jnp
from jax import lax
from jax.experimental import pallas as pl
from jax.experimental.pallas import tpu as pltpu
from jax.sharding import PartitionSpec as P

LONG = 8
MESH = pl.DeviceIdType.MESH
LOG2E = 1.4426950408889634
NEG = -1e30
F32 = jnp.float32
BF16 = jnp.bfloat16


def rows_of(index, count):
    return pl.ds(pl.multiple_of(index * count, count), count)


def softmax_grads(keys, vals, quer, grad, mask, scale):
    nt = (((1,), (1,)), ((), ()))
    scores = lax.dot_general(keys, quer, nt, preferred_element_type=F32)
    scores = jnp.where(mask, scores, NEG)
    prob_grad = lax.dot_general(vals, grad, nt, preferred_element_type=F32)
    top = jnp.max(scores, axis=0, keepdims=True)
    unnorm = jnp.exp2((scores - top) * (scale * LOG2E))
    probs = unnorm * (1.0 / jnp.sum(unnorm, axis=0, keepdims=True))
    delta = jnp.sum(probs * prob_grad, axis=0, keepdims=True)
    dscore = (probs * (prob_grad - delta)).astype(BF16)
    dv = jnp.dot(probs.astype(BF16), grad, preferred_element_type=F32)
    dk = jnp.dot(dscore, quer, preferred_element_type=F32) * scale
    dq = (
        lax.dot_general(dscore, keys, (((0,), (0,)), ((), ())), preferred_element_type=F32)
        * scale
    )
    return dq, dk, dv


def kernel(
    n, cells, cell, long_cells, heads,
    info, q_ref, k_ref, v_ref, g_ref,
    dq_ref, dkv_ref,
    in1, out1, in2, out2, in3, out3, in4, out4,
    prev, dprev, dprev_rx, own, own_rx,
    send_sem, recv_sem, sib_send, sib_recv,
):
    me = lax.axis_index("dp")
    core = lax.axis_index("section")
    sib = 1 - core
    crow = cell * heads
    scale = q_ref.shape[-1] ** -0.5
    INV, BND = cells, cells + n

    barrier = pltpu.get_barrier_semaphore()

    def greet(k, _):
        pl.semaphore_signal(
            barrier, inc=1, device_id={"dp": lax.rem(me + k, n)}, device_id_type=MESH
        )
        return 0

    lax.fori_loop(1, n, greet, 0)
    pl.semaphore_signal(barrier, inc=1, device_id={"section": sib}, device_id_type=MESH)

    def hop(phase, src, dst, peer, slot):
        return pltpu.make_async_remote_copy(
            src_ref=src.at[peer],
            dst_ref=dst.at[slot],
            send_sem=send_sem.at[phase, peer],
            recv_sem=recv_sem.at[phase, slot],
            device_id={"dp": peer},
            device_id_type=MESH,
        )

    def arrived(phase, src, dst, peer):
        hop(phase, src, dst, peer, peer).wait_recv()

    def sent(phase, src, dst):
        def body(k, _):
            peer = lax.rem(me + k, n)
            hop(phase, src, dst, peer, peer).wait_send()
            return 0

        lax.fori_loop(1, n, body, 0)

    def swap(which, src, dst):
        return pltpu.make_async_remote_copy(
            src_ref=src,
            dst_ref=dst,
            send_sem=sib_send.at[which],
            recv_sem=sib_recv.at[which],
            device_id={"section": sib},
            device_id_type=MESH,
        )

    first_row = lax.broadcasted_iota(jnp.int32, (cell, k_ref.shape[-1]), 0) == 0

    def fill(d, _):
        at = info[INV + d]
        pos = jnp.maximum(at, 0)
        block = jnp.where(core == 0, k_ref[pos], v_ref[pos]).astype(F32)
        block = jnp.where(first_row, info[BND + pos].astype(F32), block)
        out1[d] = jnp.where(at >= 0, block, 0.0).astype(BF16)
        return 0

    lax.fori_loop(0, n, fill, 0)
    in1[me] = out1[me]

    pl.semaphore_wait(barrier, n)

    def launch1(k, _):
        hop(0, out1, in1, lax.rem(me + k, n), me).start()
        return 0

    lax.fori_loop(1, n, launch1, 0)

    long_len = long_cells * cell
    own[...] = jnp.zeros(own.shape, F32)
    dq_ref[long_cells * crow :, :] = jnp.zeros(
        (dq_ref.shape[0] - long_cells * crow, dq_ref.shape[1]), BF16
    )
    flat = (long_len, k_ref.shape[-1])
    long_key = lax.broadcasted_iota(jnp.int32, (long_len, crow), 0)
    long_query = lax.broadcasted_iota(jnp.int32, (long_len, crow), 1) // heads

    def long_step(c, _):
        rows = rows_of(c, crow)
        dq, dk, dv = softmax_grads(
            k_ref[:long_cells].reshape(flat), v_ref[:long_cells].reshape(flat),
            q_ref[rows, :], g_ref[rows, :],
            long_key <= long_query + c * cell, scale,
        )
        dq_ref[rows, :] = dq.astype(BF16)
        own[0, :long_cells] += dk.reshape(long_cells, cell, -1)
        own[1, :long_cells] += dv.reshape(long_cells, cell, -1)
        return 0

    lax.fori_loop(0, long_cells, long_step, 0)

    def hub(r, last):
        @pl.when(r != me)
        def _():
            arrived(0, out1, in1, r)

        out2[r] = last.astype(BF16)

        @pl.when(r != me)
        def _():
            hop(1, out2, in2, r, me).start()

        block = in1[r].astype(F32)
        return jnp.where(block[0:1, :] > 0.0, block, last)

    lax.fori_loop(0, n, hub, jnp.zeros((cell, k_ref.shape[-1]), F32))
    in2[me] = out2[me]

    def take2(k, _):
        arrived(1, out2, in2, lax.rem(me + k, n))
        return 0

    lax.fori_loop(1, n, take2, 0)

    def gather(c, _):
        pos = jnp.maximum(info[c], 0)
        prev[core, c] = in2[pos]
        return 0

    lax.fori_loop(0, cells, gather, 0)
    swap_prev = swap(0, prev.at[core], prev.at[core])
    swap_prev.start()
    swap_prev.wait()

    win_key = lax.broadcasted_iota(jnp.int32, (2 * cell, crow), 0)
    win_query = lax.broadcasted_iota(jnp.int32, (2 * cell, crow), 1) // heads
    causal = win_key <= win_query + cell

    def stream_step(c, _):
        qrows = rows_of(c, crow)
        prev_key = prev[0, c]
        keys = jnp.concatenate([prev_key, k_ref[c]], axis=0)
        vals = jnp.concatenate([prev[1, c], v_ref[c]], axis=0)
        mark = prev_key.astype(F32)[0:1, :]
        mark = jnp.concatenate([mark] * (crow // mark.shape[1]), axis=1)
        bound = info[BND + c]
        start = jnp.where(mark > 0.0, mark.astype(jnp.int32), cell)
        low = jnp.where(win_query[0:1, :] < bound, start, bound + cell)
        mask = (win_key >= low) & causal
        dq, dk, dv = softmax_grads(keys, vals, q_ref[qrows, :], g_ref[qrows, :], mask, scale)
        kept = info[c] < 0
        dq_ref[qrows, :] = jnp.where(kept, dq_ref[qrows, :].astype(F32), dq).astype(BF16)
        own[0, c] = jnp.where(kept, own[0, c], dk[cell:])
        own[1, c] = jnp.where(kept, own[1, c], dv[cell:])
        dprev[0, c] = dk[:cell].astype(BF16)
        dprev[1, c] = dv[:cell].astype(BF16)
        return 0

    lax.fori_loop(0, cells, stream_step, 0)

    swap_dprev = swap(1, dprev.at[sib], dprev_rx)
    swap_dprev.start()
    swap_own = swap(2, own.at[sib], own_rx)
    swap_own.start()
    swap_dprev.wait()

    def add(c, _):
        dprev[core, c] = (dprev[core, c].astype(F32) + dprev_rx[c].astype(F32)).astype(BF16)
        return 0

    lax.fori_loop(0, cells, add, 0)

    def fill3(k, _):
        d = lax.rem(me + k, n)
        pos = jnp.maximum(info[INV + d], 0)
        out3[d] = dprev[core, pos]

        @pl.when(k != 0)
        def _():
            hop(2, out3, in3, d, me).start()

        return 0

    lax.fori_loop(0, n, fill3, 0)
    in3[me] = out3[me]

    def hub_back(k, later):
        r = n - 1 - k

        @pl.when(r != me)
        def _():
            arrived(2, out3, in3, r)

        out4[r] = later.astype(BF16)

        @pl.when(r != me)
        def _():
            hop(3, out4, in4, r, me).start()

        marks = in1[r].astype(F32)
        block = in3[r].astype(F32)
        return jnp.where(marks[0:1, :] > 0.0, block, later)

    lax.fori_loop(0, n, hub_back, jnp.zeros((cell, k_ref.shape[-1]), F32))
    in4[me] = out4[me]

    def take4(k, _):
        arrived(3, out4, in4, lax.rem(me + k, n))
        return 0

    lax.fori_loop(1, n, take4, 0)
    swap_own.wait()

    def finish(c, _):
        plan = info[c]
        back = in4[jnp.maximum(plan, 0)].astype(F32)
        total = own[core, c] + own_rx[c] + jnp.where(plan >= 0, back, 0.0)
        dkv_ref[core, c] = total.astype(BF16)
        return 0

    lax.fori_loop(0, cells, finish, 0)
    swap_out = swap(3, dkv_ref.at[core], dkv_ref.at[core])
    swap_out.start()
    sent(0, out1, in1)
    sent(1, out2, in2)
    sent(2, out3, in3)
    sent(3, out4, in4)
    swap_out.wait()


def on_device(n, query_heads, key_heads, value_heads, attend_grad, doc_ids, cell_plan):
    tokens, _, heads, width = query_heads.shape
    cells = cell_plan.shape[0]
    cell = tokens // cells
    doc = doc_ids.reshape(cells, cell)
    bound = jnp.sum((doc == doc[:, :1]).astype(jnp.int32), axis=1)
    match = cell_plan[None, :] == jnp.arange(n, dtype=jnp.int32)[:, None]
    inverse = jnp.sum(jnp.where(match, jnp.arange(cells, dtype=jnp.int32)[None, :] + 1, 0), axis=1) - 1
    info = jnp.concatenate([cell_plan, inverse, bound])

    slots = pltpu.VMEM((n, cell, width), BF16)
    vmem = pl.BlockSpec(memory_space=pltpu.VMEM)
    dq, dkv = pl.pallas_call(
        functools.partial(kernel, n, cells, cell, LONG, heads),
        out_shape=(
            jax.ShapeDtypeStruct((tokens * heads, width), BF16),
            jax.ShapeDtypeStruct((2, cells, cell, width), BF16),
        ),
        in_specs=[pl.BlockSpec(memory_space=pltpu.SMEM)] + [vmem] * 4,
        out_specs=(vmem, vmem),
        scratch_shapes=[slots] * 8
        + [
            pltpu.VMEM((2, cells, cell, width), BF16),
            pltpu.VMEM((2, cells, cell, width), BF16),
            pltpu.VMEM((cells, cell, width), BF16),
            pltpu.VMEM((2, cells, cell, width), F32),
            pltpu.VMEM((cells, cell, width), F32),
            pltpu.SemaphoreType.DMA((4, n)),
            pltpu.SemaphoreType.DMA((4, n)),
            pltpu.SemaphoreType.DMA((4,)),
            pltpu.SemaphoreType.DMA((4,)),
        ],
        compiler_params=pltpu.CompilerParams(
            collective_id=0, has_side_effects=True, vmem_limit_bytes=48 * 2**20
        ),
    )(
        info,
        query_heads.reshape(tokens * heads, width),
        key_heads.reshape(cells, cell, width),
        value_heads.reshape(cells, cell, width),
        attend_grad.reshape(tokens * heads, width),
    )
    return (
        dq.reshape(tokens, 1, heads, width),
        dkv[0].reshape(tokens, 1, width),
        dkv[1].reshape(tokens, 1, width),
    )


def solution(mesh):
    wide = P("dp", "tensor", "section", None)
    narrow = P("dp", "tensor", None)
    return jax.shard_map(
        functools.partial(on_device, mesh.shape["dp"]),
        mesh=mesh,
        in_specs=(wide, narrow, narrow, wide, P("dp"), P("dp")),
        out_specs=(wide, narrow, narrow),
        check_vma=False,
    )
```

```python
import functools

import jax
import jax.numpy as jnp
from jax import lax
from jax.experimental import pallas as pl
from jax.experimental.pallas import tpu as pltpu
from jax.sharding import PartitionSpec as P

LONG = 8
CHUNKS = 4
MESH = pl.DeviceIdType.MESH
LOG2E = 1.4426950408889634
NEG = -1e30
F32 = jnp.float32
BF16 = jnp.bfloat16
NT = (((1,), (1,)), ((), ()))
TN = (((0,), (0,)), ((), ()))


def rows_of(index, count):
    return pl.ds(pl.multiple_of(index * count, count), count)


def dot(a, b, dims=(((1,), (0,)), ((), ()))):
    return lax.dot_general(a, b, dims, preferred_element_type=F32)


def softmax_grads(keys, vals, quer, grad, mask, scale):
    scores = jnp.where(mask, dot(keys, quer, NT), NEG)
    prob_grad = dot(vals, grad, NT)
    top = jnp.max(scores, axis=0, keepdims=True)
    unnorm = jnp.exp2((scores - top) * (scale * LOG2E))
    probs = unnorm * (1.0 / jnp.sum(unnorm, axis=0, keepdims=True))
    delta = jnp.sum(probs * prob_grad, axis=0, keepdims=True)
    dscore = (probs * (prob_grad - delta)).astype(BF16)
    dv = dot(probs.astype(BF16), grad)
    dk = dot(dscore, quer) * scale
    dq = dot(dscore, keys, TN) * scale
    return dq, dk, dv


def kernel(
    n, cells, cell, long_cells, heads,
    plan_hbm, doc_hbm, q_hbm, k_hbm, v_hbm, g_hbm,
    dq_ref, dkv_ref,
    plan, doc, inverse, bound, q_ref, k_ref, v_ref, g_ref,
    in1, out1, in2, out2, in3, out3, in4, out4,
    prev, dprev, dprev_rx, own, own_rx, stats, dscore_prev,
    load_sem, send_sem, slot_sem, all_sem, sib_send, sib_recv,
):
    me = lax.axis_index("dp")
    core = lax.axis_index("section")
    sib = 1 - core
    crow = cell * heads
    width = q_ref.shape[-1]
    scale = width ** -0.5
    chunk = cells // CHUNKS

    loads = [
        pltpu.make_async_copy(src, dst, load_sem.at[i])
        for i, (src, dst) in enumerate(
            ((plan_hbm, plan), (doc_hbm, doc), (k_hbm, k_ref), (v_hbm, v_ref), (q_hbm, q_ref), (g_hbm, g_ref))
        )
    ]
    for load in loads:
        load.start()

    barrier = pltpu.get_barrier_semaphore()

    def greet(k, _):
        pl.semaphore_signal(
            barrier, inc=1, device_id={"dp": lax.rem(me + k, n)}, device_id_type=MESH
        )
        return 0

    lax.fori_loop(1, n, greet, 0)
    pl.semaphore_signal(barrier, inc=1, device_id={"section": sib}, device_id_type=MESH)

    def hop(phase, src, dst, peer, slot, recv):
        return pltpu.make_async_remote_copy(
            src_ref=src.at[peer],
            dst_ref=dst.at[slot],
            send_sem=send_sem.at[phase],
            recv_sem=recv,
            device_id={"dp": peer},
            device_id_type=MESH,
        )

    def whole(phase, src, dst):
        return pltpu.make_async_remote_copy(
            src_ref=src.at[pl.ds(0, n - 1)],
            dst_ref=dst.at[pl.ds(0, n - 1)],
            send_sem=send_sem.at[phase],
            recv_sem=all_sem.at[phase],
            device_id={"section": sib},
            device_id_type=MESH,
        )

    def swap(which, src, dst):
        return pltpu.make_async_remote_copy(
            src_ref=src,
            dst_ref=dst,
            send_sem=sib_send.at[which],
            recv_sem=sib_recv.at[which],
            device_id={"section": sib},
            device_id_type=MESH,
        )

    loads[0].wait()
    loads[1].wait()

    def bounds(c, _):
        base = c * cell
        lead = doc[base]
        last = jnp.int32(0)
        step = cell // 2
        while step:
            last = jnp.where(doc[base + last + step] == lead, last + step, last)
            step //= 2
        bound[c] = last + 1
        return 0

    lax.fori_loop(0, cells, bounds, 0, unroll=4)

    def invert(d, _):
        at = jnp.int32(-1)
        for c in range(cells):
            at = jnp.where(plan[c] == d, c, at)
        inverse[d] = at
        return 0

    lax.fori_loop(0, n, invert, 0, unroll=2)

    loads[2].wait()
    loads[3].wait()
    first_row = lax.broadcasted_iota(jnp.int32, (cell, width), 0) == 0

    def fill(d, _):
        at = inverse[d]
        pos = jnp.maximum(at, 0)
        block = jnp.where(core == 0, k_ref[pos], v_ref[pos]).astype(F32)
        block = jnp.where(first_row, bound[pos].astype(F32), block)
        out1[d] = jnp.where(at >= 0, block, 0.0).astype(BF16)
        return 0

    lax.fori_loop(0, n, fill, 0, unroll=4)
    in1[me] = out1[me]

    pl.semaphore_wait(barrier, n)

    def launch1(k, _):
        hop(0, out1, in1, lax.rem(me + k, n), me, slot_sem.at[0, me]).start()
        return 0

    lax.fori_loop(1, n, launch1, 0)

    loads[4].wait()
    loads[5].wait()
    long_len = long_cells * cell
    own[...] = jnp.zeros(own.shape, F32)
    dq_ref[long_cells * crow :, :] = jnp.zeros(
        (dq_ref.shape[0] - long_cells * crow, dq_ref.shape[1]), BF16
    )
    flat = (long_len, width)
    long_key = lax.broadcasted_iota(jnp.int32, (long_len, crow), 0)
    long_query = lax.broadcasted_iota(jnp.int32, (long_len, crow), 1) // heads

    def long_step(c, _):
        rows = rows_of(c, crow)
        dq, dk, dv = softmax_grads(
            k_ref[:long_cells].reshape(flat), v_ref[:long_cells].reshape(flat),
            q_ref[rows, :], g_ref[rows, :],
            long_key <= long_query + c * cell, scale,
        )
        dq_ref[rows, :] = dq.astype(BF16)
        own[0, :long_cells] += dk.reshape(long_cells, cell, -1)
        own[1, :long_cells] += dv.reshape(long_cells, cell, -1)
        return 0

    lax.fori_loop(0, long_cells, long_step, 0)

    def hub(r, last):
        @pl.when(r != me)
        def _():
            hop(0, out1, in1, r, r, slot_sem.at[0, r]).wait_recv()

        out2[r] = last.astype(BF16)

        @pl.when(r != me)
        def _():
            hop(1, out2, in2, r, me, all_sem.at[1]).start()

        block = in1[r].astype(F32)
        return jnp.where(block[0:1, :] > 0.0, block, last)

    lax.fori_loop(0, n, hub, jnp.zeros((cell, width), F32))
    in2[me] = out2[me]
    whole(0, out1, in1).wait_send()

    key_at = lax.broadcasted_iota(jnp.int32, (cell, crow), 0)
    query_at = lax.broadcasted_iota(jnp.int32, (cell, crow), 1) // heads
    causal = key_at <= query_at
    query_row = query_at[0:1, :]

    def own_block(c):
        rows = rows_of(c, crow)
        low = jnp.where(query_row < bound[c], 0, bound[c])
        scores = jnp.where(causal & (key_at >= low), dot(k_ref[c], q_ref[rows, :], NT), NEG)
        return scores, dot(v_ref[c], g_ref[rows, :], NT)

    def own_stats(c, _):
        scores, prob_grad = own_block(c)
        top = jnp.max(scores, axis=0, keepdims=True)
        unnorm = jnp.exp2((scores - top) * (scale * LOG2E))
        stats[c, 0:1] = top
        stats[c, 1:2] = jnp.sum(unnorm, axis=0, keepdims=True)
        stats[c, 2:3] = jnp.sum(unnorm * prob_grad, axis=0, keepdims=True)
        return 0

    lax.fori_loop(0, cells, own_stats, 0, unroll=4)

    whole(1, out2, in2).wait_recv()
    swaps = []
    for part in range(CHUNKS):
        span = pl.ds(part * chunk, chunk)
        for c in range(part * chunk, (part + 1) * chunk):
            prev[core, c] = in2[jnp.maximum(plan[c], 0)]
        swaps.append(swap(part, prev.at[core, span], prev.at[core, span]))
        swaps[-1].start()

    def cross(c, _):
        rows = rows_of(c, crow)
        quer, grad = q_ref[rows, :], g_ref[rows, :]
        prev_key = prev[0, c]
        mark = prev_key.astype(F32)[0:1, :]
        mark = jnp.concatenate([mark] * (crow // width), axis=1)
        mark = jnp.where(mark > 0.0, mark.astype(jnp.int32), cell)
        low = jnp.where(query_row < bound[c], mark, cell)
        scores = jnp.where(key_at >= low, dot(prev_key, quer, NT), NEG)
        prob_grad = dot(prev[1, c], grad, NT)
        own_top = stats[c, 0:1]
        top = jnp.maximum(jnp.max(scores, axis=0, keepdims=True), own_top)
        unnorm = jnp.exp2((scores - top) * (scale * LOG2E))
        shrink = jnp.exp2((own_top - top) * (scale * LOG2E))
        inv = 1.0 / (jnp.sum(unnorm, axis=0, keepdims=True) + shrink * stats[c, 1:2])
        delta = inv * (
            jnp.sum(unnorm * prob_grad, axis=0, keepdims=True) + shrink * stats[c, 2:3]
        )
        probs = unnorm * inv
        dscore = (probs * (prob_grad - delta)).astype(BF16)
        stats[c, 0:1] = top
        stats[c, 1:2] = inv
        stats[c, 2:3] = delta
        dscore_prev[c] = dscore
        dprev[0, c] = (dot(dscore, quer) * scale).astype(BF16)
        dprev[1, c] = dot(probs.astype(BF16), grad).astype(BF16)
        return 0

    back = []
    for part in range(CHUNKS):
        span = pl.ds(part * chunk, chunk)
        swaps[part].wait_recv()
        lax.fori_loop(part * chunk, (part + 1) * chunk, cross, 0, unroll=True)
        back.append(swap(CHUNKS + part, dprev.at[sib, span], dprev_rx.at[span]))
        back[-1].start()
    for part in range(CHUNKS):
        back[part].wait_recv()

    def fill3(k, _):
        d = lax.rem(me + k, n)
        pos = jnp.maximum(inverse[d], 0)
        out3[d] = (dprev[core, pos].astype(F32) + dprev_rx[pos].astype(F32)).astype(BF16)

        @pl.when(k != 0)
        def _():
            hop(2, out3, in3, d, me, slot_sem.at[1, me]).start()

        return 0

    lax.fori_loop(0, n, fill3, 0)
    in3[me] = out3[me]
    whole(1, out2, in2).wait_send()

    def own_grads(c, _):
        rows = rows_of(c, crow)
        quer, grad = q_ref[rows, :], g_ref[rows, :]
        scores, prob_grad = own_block(c)
        probs = jnp.exp2((scores - stats[c, 0:1]) * (scale * LOG2E)) * stats[c, 1:2]
        dscore = (probs * (prob_grad - stats[c, 2:3])).astype(BF16)
        dv = dot(probs.astype(BF16), grad)
        dk = dot(dscore, quer) * scale
        dq = (dot(dscore, k_ref[c], TN) + dot(dscore_prev[c], prev[0, c], TN)) * scale
        kept = plan[c] < 0
        dq_ref[rows, :] = jnp.where(kept, dq_ref[rows, :].astype(F32), dq).astype(BF16)
        own[0, c] = jnp.where(kept, own[0, c], dk)
        own[1, c] = jnp.where(kept, own[1, c], dv)
        return 0

    lax.fori_loop(0, cells, own_grads, 0, unroll=2)
    swap_own = swap(2 * CHUNKS, own.at[sib], own_rx)
    swap_own.start()

    def hub_back(k, later):
        r = n - 1 - k

        @pl.when(r != me)
        def _():
            hop(2, out3, in3, r, r, slot_sem.at[1, r]).wait_recv()

        out4[r] = later.astype(BF16)

        @pl.when(r != me)
        def _():
            hop(3, out4, in4, r, me, all_sem.at[3]).start()

        marks = in1[r].astype(F32)
        return jnp.where(marks[0:1, :] > 0.0, in3[r].astype(F32), later)

    lax.fori_loop(0, n, hub_back, jnp.zeros((cell, width), F32))
    in4[me] = out4[me]
    whole(2, out3, in3).wait_send()
    for part in range(CHUNKS):
        swaps[part].wait_send()
        back[part].wait_send()
    swap_own.wait()
    whole(3, out4, in4).wait_recv()

    last = []
    for part in range(CHUNKS):
        span = pl.ds(part * chunk, chunk)
        for c in range(part * chunk, (part + 1) * chunk):
            home = plan[c]
            came = in4[jnp.maximum(home, 0)].astype(F32)
            total = own[core, c] + own_rx[c] + jnp.where(home >= 0, came, 0.0)
            dkv_ref[core, c] = total.astype(BF16)
        last.append(swap(2 * CHUNKS + 1 + part, dkv_ref.at[core, span], dkv_ref.at[core, span]))
        last[-1].start()
    whole(3, out4, in4).wait_send()
    for part in range(CHUNKS):
        last[part].wait()


def on_device(n, query_heads, key_heads, value_heads, attend_grad, doc_ids, cell_plan):
    tokens, _, heads, width = query_heads.shape
    cells = cell_plan.shape[0]
    cell = tokens // cells
    crow = cell * heads

    slots = pltpu.VMEM((n, cell, width), BF16)
    pair = pltpu.VMEM((2, cells, cell, width), BF16)
    vmem = pl.BlockSpec(memory_space=pltpu.VMEM)
    hbm = pl.BlockSpec(memory_space=pl.ANY)
    wide = pltpu.VMEM((tokens * heads, width), BF16)
    narrow = pltpu.VMEM((cells, cell, width), BF16)
    n_swaps = 3 * CHUNKS + 1
    dq, dkv = pl.pallas_call(
        functools.partial(kernel, n, cells, cell, LONG, heads),
        out_shape=(
            jax.ShapeDtypeStruct((tokens * heads, width), BF16),
            jax.ShapeDtypeStruct((2, cells, cell, width), BF16),
        ),
        in_specs=[hbm] * 6,
        out_specs=(vmem, vmem),
        scratch_shapes=[
            pltpu.SMEM((cells,), jnp.int32),
            pltpu.SMEM((tokens,), jnp.int32),
            pltpu.SMEM((n,), jnp.int32),
            pltpu.SMEM((cells,), jnp.int32),
            wide, narrow, narrow, wide,
        ]
        + [slots] * 8
        + [
            pair, pair, narrow,
            pltpu.VMEM((2, cells, cell, width), F32),
            pltpu.VMEM((cells, cell, width), F32),
            pltpu.VMEM((cells, 8, crow), F32),
            pltpu.VMEM((cells, cell, crow), BF16),
            pltpu.SemaphoreType.DMA((6,)),
            pltpu.SemaphoreType.DMA((4,)),
            pltpu.SemaphoreType.DMA((2, n)),
            pltpu.SemaphoreType.DMA((4,)),
            pltpu.SemaphoreType.DMA((n_swaps,)),
            pltpu.SemaphoreType.DMA((n_swaps,)),
        ],
        compiler_params=pltpu.CompilerParams(
            collective_id=0, has_side_effects=True, vmem_limit_bytes=48 * 2**20
        ),
    )(
        cell_plan,
        doc_ids,
        query_heads.reshape(tokens * heads, width),
        key_heads.reshape(cells, cell, width),
        value_heads.reshape(cells, cell, width),
        attend_grad.reshape(tokens * heads, width),
    )
    return (
        dq.reshape(tokens, 1, heads, width),
        dkv[0].reshape(tokens, 1, width),
        dkv[1].reshape(tokens, 1, width),
    )


def solution(mesh):
    wide = P("dp", "tensor", "section", None)
    narrow = P("dp", "tensor", None)
    return jax.shard_map(
        functools.partial(on_device, mesh.shape["dp"]),
        mesh=mesh,
        in_specs=(wide, narrow, narrow, wide, P("dp"), P("dp")),
        out_specs=(wide, narrow, narrow),
        check_vma=False,
    )
```

```python
import functools

import jax
import jax.numpy as jnp
from jax import lax
from jax.experimental import pallas as pl
from jax.experimental.pallas import tpu as pltpu
from jax.sharding import PartitionSpec as P

LONG = 8
CHUNKS = 4
PARTS = 4
MESH = pl.DeviceIdType.MESH
LOG2E = 1.4426950408889634
NEG = -1e30
F32 = jnp.float32
BF16 = jnp.bfloat16
NT = (((1,), (1,)), ((), ()))
TN = (((0,), (0,)), ((), ()))


def rows_of(index, count):
    return pl.ds(pl.multiple_of(index * count, count), count)


def dot(a, b, dims=(((1,), (0,)), ((), ()))):
    return lax.dot_general(a, b, dims, preferred_element_type=F32)


def softmax_grads(keys, vals, quer, grad, mask, scale):
    scores = jnp.where(mask, dot(keys, quer, NT), NEG)
    prob_grad = dot(vals, grad, NT)
    top = jnp.max(scores, axis=0, keepdims=True)
    unnorm = jnp.exp2((scores - top) * (scale * LOG2E))
    probs = unnorm * (1.0 / jnp.sum(unnorm, axis=0, keepdims=True))
    delta = jnp.sum(probs * prob_grad, axis=0, keepdims=True)
    dscore = (probs * (prob_grad - delta)).astype(BF16)
    dv = dot(probs.astype(BF16), grad)
    dk = dot(dscore, quer) * scale
    dq = dot(dscore, keys, TN) * scale
    return dq, dk, dv


def kernel(
    n, cells, cell, long_cells, heads,
    plan_hbm, doc_hbm, q_hbm, k_hbm, v_hbm, g_hbm,
    dq_hbm, dk_hbm, dv_hbm,
    plan, doc, flags, rank, slot, inverse, bound, q_ref, k_ref, v_ref, g_ref, dq_ref, total_ref, marked,
    in1, out1, in2, out2, in3, out3, in4, out4,
    prev, dprev, dprev_rx, own, own_rx, stats, dscore_prev,
    load_sem, send_sem, slot_sem, all_sem, sib_send, sib_recv, store_sem,
):
    me = lax.axis_index("dp")
    core = lax.axis_index("section")
    sib = 1 - core
    crow = cell * heads
    width = q_ref.shape[-1]
    scale = width ** -0.5
    chunk = cells // CHUNKS
    part_rows = cell // PARTS
    n_slots = 3 * n // 4
    deal = n_slots * PARTS // n

    loads = [
        pltpu.make_async_copy(src, dst, load_sem.at[i])
        for i, (src, dst) in enumerate(
            ((plan_hbm, plan), (doc_hbm, doc), (k_hbm, k_ref), (v_hbm, v_ref), (q_hbm, q_ref), (g_hbm, g_ref))
        )
    ]
    for load in loads:
        load.start()

    barrier = pltpu.get_barrier_semaphore()

    def greet(k, _):
        pl.semaphore_signal(
            barrier, inc=1, device_id={"dp": lax.rem(me + k, n)}, device_id_type=MESH
        )
        return 0

    lax.fori_loop(1, n, greet, 0)
    pl.semaphore_signal(barrier, inc=1, device_id={"section": sib}, device_id_type=MESH)

    def hop(phase, src, dst, peer, place, recv):
        return pltpu.make_async_remote_copy(
            src_ref=src.at[pl.ds(peer * deal, deal)],
            dst_ref=dst.at[pl.ds(place * deal, deal)],
            send_sem=send_sem.at[phase],
            recv_sem=recv,
            device_id={"dp": peer},
            device_id_type=MESH,
        )

    def whole(phase, src, dst):
        return pltpu.make_async_remote_copy(
            src_ref=src.at[pl.ds(0, (n - 1) * deal)],
            dst_ref=dst.at[pl.ds(0, (n - 1) * deal)],
            send_sem=send_sem.at[phase],
            recv_sem=all_sem.at[phase],
            device_id={"section": sib},
            device_id_type=MESH,
        )

    def swap(which, src, dst):
        return pltpu.make_async_remote_copy(
            src_ref=src,
            dst_ref=dst,
            send_sem=sib_send.at[which],
            recv_sem=sib_recv.at[which],
            device_id={"section": sib},
            device_id_type=MESH,
        )

    loads[0].wait()
    loads[1].wait()

    def bounds(c, _):
        base = c * cell
        lead = doc[base]
        last = jnp.int32(0)
        step = cell // 2
        while step:
            last = jnp.where(doc[base + last + step] == lead, last + step, last)
            step //= 2
        bound[c] = last + 1
        return 0

    lax.fori_loop(0, cells, bounds, 0, unroll=4)

    for i in range(flags.shape[1]):
        flags[me, i] = plan[0]

    loads[2].wait()
    loads[3].wait()
    row_at = lax.broadcasted_iota(jnp.int32, (cell, width), 0)

    def mark(c, _):
        block = jnp.where(core == 0, k_ref[c], v_ref[c]).astype(F32)
        moved = block
        for i in range(1, PARTS):
            moved = jnp.where(row_at == i, block[i * part_rows : i * part_rows + 1, :], moved)
        moved = jnp.where(row_at % part_rows == 0, bound[c].astype(F32), moved)
        marked[c] = moved.astype(BF16)
        return 0

    lax.fori_loop(0, cells, mark, 0, unroll=4)

    pl.semaphore_wait(barrier, n)

    def tell(k, _):
        pltpu.make_async_remote_copy(
            src_ref=flags.at[me],
            dst_ref=flags.at[me],
            send_sem=send_sem.at[4],
            recv_sem=all_sem.at[0],
            device_id={"dp": lax.rem(me + k, n)},
            device_id_type=MESH,
        ).start()
        return 0

    lax.fori_loop(1, n, tell, 0)
    told = pltpu.make_async_remote_copy(
        src_ref=flags.at[pl.ds(0, n - 1)],
        dst_ref=flags.at[pl.ds(0, n - 1)],
        send_sem=send_sem.at[4],
        recv_sem=all_sem.at[0],
        device_id={"section": sib},
        device_id_type=MESH,
    )
    told.wait_recv()

    keepers = jnp.int32(0)
    for d in range(n):
        rank[d] = d - keepers
        keepers += jnp.where(flags[d, 0] < 0, 1, 0)
    for c in range(cells):
        slot[c] = jnp.where(plan[c] >= 0, rank[jnp.maximum(plan[c], 0)], -1)

    def fill(j, _):
        at = jnp.int32(-1)
        for c in range(cells):
            at = jnp.where(slot[c] == j, c, at)
        inverse[j] = at
        block = jnp.where(at >= 0, marked[jnp.maximum(at, 0)], jnp.zeros((cell, width), BF16))
        out1[pl.ds(j * PARTS, PARTS)] = block.reshape(PARTS, part_rows, width)
        return 0

    lax.fori_loop(0, n_slots, fill, 0, unroll=2)

    def mine(ref):
        return ref[pl.ds(me * deal, deal)]

    in1[pl.ds(me * deal, deal)] = mine(out1)

    def launch1(k, _):
        hop(0, out1, in1, lax.rem(me + k, n), me, slot_sem.at[0, me]).start()
        return 0

    lax.fori_loop(1, n, launch1, 0)

    loads[4].wait()
    loads[5].wait()
    long_len = long_cells * cell
    own[...] = jnp.zeros(own.shape, F32)
    dq_ref[long_cells * crow :, :] = jnp.zeros(
        (dq_ref.shape[0] - long_cells * crow, dq_ref.shape[1]), BF16
    )
    flat = (long_len, width)
    long_key = lax.broadcasted_iota(jnp.int32, (long_len, crow), 0)
    long_query = lax.broadcasted_iota(jnp.int32, (long_len, crow), 1) // heads

    def long_step(c, _):
        rows = rows_of(c, crow)
        dq, dk, dv = softmax_grads(
            k_ref[:long_cells].reshape(flat), v_ref[:long_cells].reshape(flat),
            q_ref[rows, :], g_ref[rows, :],
            long_key <= long_query + c * cell, scale,
        )
        dq_ref[rows, :] = dq.astype(BF16)
        own[0, :long_cells] += dk.reshape(long_cells, cell, -1)
        own[1, :long_cells] += dv.reshape(long_cells, cell, -1)
        return 0

    lax.fori_loop(0, long_cells, long_step, 0)

    def hub(r, last):
        @pl.when(r != me)
        def _():
            hop(0, out1, in1, r, r, slot_sem.at[0, r]).wait_recv()

        out2[pl.ds(r * deal, deal)] = last.astype(BF16)

        @pl.when(r != me)
        def _():
            hop(1, out2, in2, r, me, all_sem.at[1]).start()

        block = in1[pl.ds(r * deal, deal)].astype(F32)
        return jnp.where(block[:, 0:1, :] > 0.0, block, last)

    lax.fori_loop(0, n, hub, jnp.zeros((deal, part_rows, width), F32))
    in2[pl.ds(me * deal, deal)] = mine(out2)
    whole(0, out1, in1).wait_send()

    key_at = lax.broadcasted_iota(jnp.int32, (cell, crow), 0)
    query_at = lax.broadcasted_iota(jnp.int32, (cell, crow), 1) // heads
    causal = key_at <= query_at
    query_row = query_at[0:1, :]
    moved_at = jnp.where(key_at < PARTS, key_at * part_rows, key_at)
    moved_at = jnp.where(key_at % part_rows == 0, -1, moved_at)

    def own_block(c):
        rows = rows_of(c, crow)
        low = jnp.where(query_row < bound[c], 0, bound[c])
        scores = jnp.where(causal & (key_at >= low), dot(k_ref[c], q_ref[rows, :], NT), NEG)
        return scores, dot(v_ref[c], g_ref[rows, :], NT)

    def own_stats(c, _):
        scores, prob_grad = own_block(c)
        top = jnp.max(scores, axis=0, keepdims=True)
        unnorm = jnp.exp2((scores - top) * (scale * LOG2E))
        stats[c, 0:1] = top
        stats[c, 1:2] = jnp.sum(unnorm, axis=0, keepdims=True)
        stats[c, 2:3] = jnp.sum(unnorm * prob_grad, axis=0, keepdims=True)
        return 0

    lax.fori_loop(0, cells, own_stats, 0, unroll=4)

    whole(1, out2, in2).wait_recv()
    swaps = []
    for part in range(CHUNKS):
        span = pl.ds(part * chunk, chunk)
        for c in range(part * chunk, (part + 1) * chunk):
            took = in2[pl.ds(jnp.maximum(slot[c], 0) * PARTS, PARTS)]
            prev[core, c] = took.reshape(cell, width)
        swaps.append(swap(part, prev.at[core, span], prev.at[core, span]))
        swaps[-1].start()

    def cross(c, _):
        rows = rows_of(c, crow)
        quer, grad = q_ref[rows, :], g_ref[rows, :]
        prev_key = prev[0, c]
        mark = prev_key.astype(F32)[0:1, :]
        mark = jnp.concatenate([mark] * (crow // width), axis=1)
        mark = jnp.where(mark > 0.0, mark.astype(jnp.int32), cell)
        low = jnp.where(query_row < bound[c], mark, cell)
        scores = jnp.where(moved_at >= low, dot(prev_key, quer, NT), NEG)
        prob_grad = dot(prev[1, c], grad, NT)
        own_top = stats[c, 0:1]
        top = jnp.maximum(jnp.max(scores, axis=0, keepdims=True), own_top)
        unnorm = jnp.exp2((scores - top) * (scale * LOG2E))
        shrink = jnp.exp2((own_top - top) * (scale * LOG2E))
        inv = 1.0 / (jnp.sum(unnorm, axis=0, keepdims=True) + shrink * stats[c, 1:2])
        delta = inv * (
            jnp.sum(unnorm * prob_grad, axis=0, keepdims=True) + shrink * stats[c, 2:3]
        )
        probs = unnorm * inv
        dscore = (probs * (prob_grad - delta)).astype(BF16)
        stats[c, 0:1] = top
        stats[c, 1:2] = inv
        stats[c, 2:3] = delta
        dscore_prev[c] = dscore
        dprev[0, c] = (dot(dscore, quer) * scale).astype(BF16)
        dprev[1, c] = dot(probs.astype(BF16), grad).astype(BF16)
        return 0

    back = []
    for part in range(CHUNKS):
        span = pl.ds(part * chunk, chunk)
        swaps[part].wait_recv()
        lax.fori_loop(part * chunk, (part + 1) * chunk, cross, 0, unroll=True)
        back.append(swap(CHUNKS + part, dprev.at[sib, span], dprev_rx.at[span]))
        back[-1].start()
    for part in range(CHUNKS):
        back[part].wait_recv()

    def fill3(j, _):
        pos = jnp.maximum(inverse[j], 0)
        block = (dprev[core, pos].astype(F32) + dprev_rx[pos].astype(F32)).astype(BF16)
        out3[pl.ds(j * PARTS, PARTS)] = block.reshape(PARTS, part_rows, width)
        return 0

    lax.fori_loop(0, n_slots, fill3, 0, unroll=2)

    def launch3(k, _):
        hop(2, out3, in3, lax.rem(me + k, n), me, slot_sem.at[1, me]).start()
        return 0

    lax.fori_loop(1, n, launch3, 0)
    in3[pl.ds(me * deal, deal)] = mine(out3)
    whole(1, out2, in2).wait_send()

    def own_grads(c, _):
        rows = rows_of(c, crow)
        quer, grad = q_ref[rows, :], g_ref[rows, :]
        scores, prob_grad = own_block(c)
        probs = jnp.exp2((scores - stats[c, 0:1]) * (scale * LOG2E)) * stats[c, 1:2]
        dscore = (probs * (prob_grad - stats[c, 2:3])).astype(BF16)
        dv = dot(probs.astype(BF16), grad)
        dk = dot(dscore, quer) * scale
        dq = (dot(dscore, k_ref[c], TN) + dot(dscore_prev[c], prev[0, c], TN)) * scale
        kept = plan[c] < 0
        dq_ref[rows, :] = jnp.where(kept, dq_ref[rows, :].astype(F32), dq).astype(BF16)
        own[0, c] = jnp.where(kept, own[0, c], dk)
        own[1, c] = jnp.where(kept, own[1, c], dv)
        return 0

    lax.fori_loop(0, cells, own_grads, 0, unroll=2)
    store_q = pltpu.make_async_copy(dq_ref, dq_hbm, store_sem.at[CHUNKS])
    store_q.start()
    swap_own = swap(2 * CHUNKS, own.at[sib], own_rx)
    swap_own.start()

    def hub_back(k, later):
        r = n - 1 - k

        @pl.when(r != me)
        def _():
            hop(2, out3, in3, r, r, slot_sem.at[1, r]).wait_recv()

        out4[pl.ds(r * deal, deal)] = later.astype(BF16)

        @pl.when(r != me)
        def _():
            hop(3, out4, in4, r, me, all_sem.at[3]).start()

        marks = in1[pl.ds(r * deal, deal)].astype(F32)
        block = in3[pl.ds(r * deal, deal)].astype(F32)
        return jnp.where(marks[:, 0:1, :] > 0.0, block, later)

    lax.fori_loop(0, n, hub_back, jnp.zeros((deal, part_rows, width), F32))
    in4[pl.ds(me * deal, deal)] = mine(out4)
    whole(2, out3, in3).wait_send()
    for part in range(CHUNKS):
        swaps[part].wait_send()
        back[part].wait_send()
    swap_own.wait()
    whole(3, out4, in4).wait_recv()

    def give(part, where):
        span = pl.ds(part * chunk, chunk)
        return (
            pltpu.make_async_copy(total_ref.at[span], where.at[span], store_sem.at[part]),
            swap(2 * CHUNKS + 1 + part, total_ref.at[span], where.at[span]),
        )

    for part in range(CHUNKS):
        for c in range(part * chunk, (part + 1) * chunk):
            came = in4[pl.ds(jnp.maximum(slot[c], 0) * PARTS, PARTS)].astype(F32).reshape(cell, width)
            back_rows = jnp.where(row_at < PARTS, 0.0, came)
            for i in range(1, PARTS):
                back_rows = jnp.where(row_at == i * part_rows, came[i : i + 1, :], back_rows)
            total = own[core, c] + own_rx[c] + jnp.where(slot[c] >= 0, back_rows, 0.0)
            total_ref[c] = total.astype(BF16)

        for which, where in ((0, dk_hbm), (1, dv_hbm)):

            @pl.when(core == which)
            def _():
                for copy in give(part, where):
                    copy.start()

    whole(3, out4, in4).wait_send()
    told.wait_send()
    store_q.wait()
    for part in range(CHUNKS):
        for which, where, other in ((0, dk_hbm, dv_hbm), (1, dv_hbm, dk_hbm)):

            @pl.when(core == which)
            def _():
                here, there = give(part, where)
                here.wait()
                there.wait_send()
                give(part, other)[1].wait_recv()


def on_device(n, query_heads, key_heads, value_heads, attend_grad, doc_ids, cell_plan):
    tokens, _, heads, width = query_heads.shape
    cells = cell_plan.shape[0]
    cell = tokens // cells
    crow = cell * heads

    n_slots = 3 * n // 4
    slots = pltpu.VMEM((n_slots * PARTS, cell // PARTS, width), BF16)
    pair = pltpu.VMEM((2, cells, cell, width), BF16)
    hbm = pl.BlockSpec(memory_space=pl.ANY)
    wide = pltpu.VMEM((tokens * heads, width), BF16)
    narrow = pltpu.VMEM((cells, cell, width), BF16)
    n_swaps = 3 * CHUNKS + 1
    dq, dk, dv = pl.pallas_call(
        functools.partial(kernel, n, cells, cell, LONG, heads),
        out_shape=(
            jax.ShapeDtypeStruct((tokens * heads, width), BF16),
            jax.ShapeDtypeStruct((cells, cell, width), BF16),
            jax.ShapeDtypeStruct((cells, cell, width), BF16),
        ),
        in_specs=[hbm] * 6,
        out_specs=[hbm] * 3,
        scratch_shapes=[
            pltpu.SMEM((cells,), jnp.int32),
            pltpu.SMEM((tokens,), jnp.int32),
            pltpu.SMEM((n, 8), jnp.int32),
            pltpu.SMEM((n,), jnp.int32),
            pltpu.SMEM((cells,), jnp.int32),
            pltpu.SMEM((n_slots,), jnp.int32),
            pltpu.SMEM((cells,), jnp.int32),
            wide, narrow, narrow, wide, wide, narrow, narrow,
        ]
        + [slots] * 8
        + [
            pair, pair, narrow,
            pltpu.VMEM((2, cells, cell, width), F32),
            pltpu.VMEM((cells, cell, width), F32),
            pltpu.VMEM((cells, 8, crow), F32),
            pltpu.VMEM((cells, cell, crow), BF16),
            pltpu.SemaphoreType.DMA((6,)),
            pltpu.SemaphoreType.DMA((5,)),
            pltpu.SemaphoreType.DMA((2, n)),
            pltpu.SemaphoreType.DMA((4,)),
            pltpu.SemaphoreType.DMA((n_swaps,)),
            pltpu.SemaphoreType.DMA((n_swaps,)),
            pltpu.SemaphoreType.DMA((CHUNKS + 1,)),
        ],
        compiler_params=pltpu.CompilerParams(
            collective_id=0, has_side_effects=True, vmem_limit_bytes=63 * 2**20
        ),
    )(
        cell_plan,
        doc_ids,
        query_heads.reshape(tokens * heads, width),
        key_heads.reshape(cells, cell, width),
        value_heads.reshape(cells, cell, width),
        attend_grad.reshape(tokens * heads, width),
    )
    return (
        dq.reshape(tokens, 1, heads, width),
        dk.reshape(tokens, 1, width),
        dv.reshape(tokens, 1, width),
    )


def solution(mesh):
    wide = P("dp", "tensor", "section", None)
    narrow = P("dp", "tensor", None)
    return jax.shard_map(
        functools.partial(on_device, mesh.shape["dp"]),
        mesh=mesh,
        in_specs=(wide, narrow, narrow, wide, P("dp"), P("dp")),
        out_specs=(wide, narrow, narrow),
        check_vma=False,
    )
```

```python
import functools

import jax
import jax.numpy as jnp
from jax import lax
from jax.experimental import pallas as pl
from jax.experimental.pallas import tpu as pltpu
from jax.sharding import PartitionSpec as P

LONG = 8
CHUNKS = 4
PARTS = 4
RING = 8
MESH = pl.DeviceIdType.MESH
LOG2E = 1.4426950408889634
NEG = -1e30
F32 = jnp.float32
BF16 = jnp.bfloat16
NT = (((1,), (1,)), ((), ()))
TN = (((0,), (0,)), ((), ()))


def rows_of(index, count):
    return pl.ds(pl.multiple_of(index * count, count), count)


def dot(a, b, dims=(((1,), (0,)), ((), ()))):
    return lax.dot_general(a, b, dims, preferred_element_type=F32)


def softmax_grads(keys, vals, quer, grad, mask, scale):
    scores = jnp.where(mask, dot(keys, quer, NT), NEG)
    prob_grad = dot(vals, grad, NT)
    top = jnp.max(scores, axis=0, keepdims=True)
    unnorm = jnp.exp2((scores - top) * (scale * LOG2E))
    probs = unnorm * (1.0 / jnp.sum(unnorm, axis=0, keepdims=True))
    delta = jnp.sum(probs * prob_grad, axis=0, keepdims=True)
    dscore = (probs * (prob_grad - delta)).astype(BF16)
    dv = dot(probs.astype(BF16), grad)
    dk = dot(dscore, quer) * scale
    dq = dot(dscore, keys, TN) * scale
    return dq, dk, dv


def kernel(
    n, cells, cell, long_cells, heads,
    plan_hbm, doc_hbm, q_hbm, k_hbm, v_hbm, g_hbm,
    dq_hbm, dkv_hbm,
    plan, doc, flags, rank, slot, inverse, bound, q_ref, k_ref, v_ref, g_ref, dq_ref, total_ref, marked,
    in1, out1, in2, out2, in3, out3, in4, out4,
    prev, dprev, dprev_rx, own, own_rx, stats, dscore_prev,
    load_sem, flag_sem, send_sem, recv_sem, sib_send, sib_recv, store_sem,
):
    me = lax.axis_index("dp")
    core = lax.axis_index("section")
    sib = 1 - core
    crow = cell * heads
    width = q_ref.shape[-1]
    scale = width ** -0.5
    chunk = cells // CHUNKS
    part_rows = cell // PARTS
    n_slots = 3 * n // 4
    deal = n_slots * PARTS // n
    ring = min(RING, n)
    lines = n // ring
    line_at, ring_at = me // ring, lax.rem(me, ring)

    steps = sorted(
        ((a, b) for a in range(ring) for b in range(lines) if a or b),
        key=lambda s: -2 * min(s[0], ring - s[0]) - min(s[1], lines - s[1]),
    )

    def peers():
        for a, b in steps:
            yield lax.rem(line_at + b, lines) * ring + lax.rem(ring_at + a, ring)

    loads = [
        pltpu.make_async_copy(src, dst, load_sem.at[i])
        for i, (src, dst) in enumerate(
            ((plan_hbm, plan), (doc_hbm, doc), (k_hbm, k_ref), (v_hbm, v_ref), (q_hbm, q_ref), (g_hbm, g_ref))
        )
    ]
    for load in loads:
        load.start()

    barrier = pltpu.get_barrier_semaphore()

    for peer in peers():
        pl.semaphore_signal(barrier, inc=1, device_id={"dp": peer}, device_id_type=MESH)
    pl.semaphore_signal(barrier, inc=1, device_id={"section": sib}, device_id_type=MESH)

    def launch(phase, part, src, dst):
        for peer in peers():
            pltpu.make_async_remote_copy(
                src_ref=src.at[peer * deal + part],
                dst_ref=dst.at[me * deal + part],
                send_sem=send_sem.at[phase, part],
                recv_sem=recv_sem.at[phase, part],
                device_id={"dp": peer},
                device_id_type=MESH,
            ).start()

    def lot(phase, part, src, dst):
        return pltpu.make_async_remote_copy(
            src_ref=src.at[pl.ds(0, n - 1)],
            dst_ref=dst.at[pl.ds(0, n - 1)],
            send_sem=send_sem.at[phase, part],
            recv_sem=recv_sem.at[phase, part],
            device_id={"section": sib},
            device_id_type=MESH,
        )

    def sent(phase, src, dst):
        for part in range(deal):
            lot(phase, part, src, dst).wait_send()

    def swap(which, src, dst):
        return pltpu.make_async_remote_copy(
            src_ref=src,
            dst_ref=dst,
            send_sem=sib_send.at[which],
            recv_sem=sib_recv.at[which],
            device_id={"section": sib},
            device_id_type=MESH,
        )

    loads[0].wait()
    loads[1].wait()

    def bounds(c, _):
        base = c * cell
        lead = doc[base]
        last = jnp.int32(0)
        step = cell // 2
        while step:
            last = jnp.where(doc[base + last + step] == lead, last + step, last)
            step //= 2
        bound[c] = last + 1
        return 0

    lax.fori_loop(0, cells, bounds, 0, unroll=4)

    for i in range(flags.shape[1]):
        flags[me, i] = plan[0]

    loads[2].wait()
    loads[3].wait()
    row_at = lax.broadcasted_iota(jnp.int32, (cell, width), 0)

    def mark(c, _):
        block = jnp.where(core == 0, k_ref[c], v_ref[c]).astype(F32)
        moved = block
        for i in range(1, PARTS):
            moved = jnp.where(row_at == i, block[i * part_rows : i * part_rows + 1, :], moved)
        moved = jnp.where(row_at % part_rows == 0, bound[c].astype(F32), moved)
        marked[c] = moved.astype(BF16)
        return 0

    lax.fori_loop(0, cells, mark, 0, unroll=4)

    pl.semaphore_wait(barrier, n)

    for peer in peers():
        pltpu.make_async_remote_copy(
            src_ref=flags.at[me],
            dst_ref=flags.at[me],
            send_sem=flag_sem.at[0],
            recv_sem=flag_sem.at[1],
            device_id={"dp": peer},
            device_id_type=MESH,
        ).start()
    told = pltpu.make_async_remote_copy(
        src_ref=flags.at[pl.ds(0, n - 1)],
        dst_ref=flags.at[pl.ds(0, n - 1)],
        send_sem=flag_sem.at[0],
        recv_sem=flag_sem.at[1],
        device_id={"section": sib},
        device_id_type=MESH,
    )
    told.wait_recv()

    keepers = jnp.int32(0)
    for d in range(n):
        rank[d] = d - keepers
        keepers += jnp.where(flags[d, 0] < 0, 1, 0)
    for c in range(cells):
        slot[c] = jnp.where(plan[c] >= 0, rank[jnp.maximum(plan[c], 0)], -1)

    def fill(j, _):
        at = jnp.int32(-1)
        for c in range(cells):
            at = jnp.where(slot[c] == j, c, at)
        inverse[j] = at
        block = jnp.where(at >= 0, marked[jnp.maximum(at, 0)], jnp.zeros((cell, width), BF16))
        out1[pl.ds(j * PARTS, PARTS)] = block.reshape(PARTS, part_rows, width)
        return 0

    lax.fori_loop(0, n_slots, fill, 0, unroll=2)

    def mine(ref):
        return ref[pl.ds(me * deal, deal)]

    in1[pl.ds(me * deal, deal)] = mine(out1)

    for part in range(deal):
        launch(0, part, out1, in1)

    loads[4].wait()
    loads[5].wait()
    long_len = long_cells * cell
    own[...] = jnp.zeros(own.shape, F32)
    dq_ref[long_cells * crow :, :] = jnp.zeros(
        (dq_ref.shape[0] - long_cells * crow, dq_ref.shape[1]), BF16
    )
    flat = (long_len, width)
    long_key = lax.broadcasted_iota(jnp.int32, (long_len, crow), 0)
    long_query = lax.broadcasted_iota(jnp.int32, (long_len, crow), 1) // heads

    def long_step(c, _):
        rows = rows_of(c, crow)
        dq, dk, dv = softmax_grads(
            k_ref[:long_cells].reshape(flat), v_ref[:long_cells].reshape(flat),
            q_ref[rows, :], g_ref[rows, :],
            long_key <= long_query + c * cell, scale,
        )
        dq_ref[rows, :] = dq.astype(BF16)
        own[0, :long_cells] += dk.reshape(long_cells, cell, -1)
        own[1, :long_cells] += dv.reshape(long_cells, cell, -1)
        return 0

    def hub(part):
        def step(r, last):
            at = r * deal + part
            out2[at] = last.astype(BF16)
            block = in1[at].astype(F32)
            return jnp.where(block[0:1, :] > 0.0, block, last)

        lax.fori_loop(0, n, step, jnp.zeros((part_rows, width), F32), unroll=8)

    def share(count, part):
        return (
            count * (deal - 2 + part) // (2 * (deal - 1)) if part else 0,
            count * (deal - 1 + part) // (2 * (deal - 1)),
        )

    lax.fori_loop(*share(long_cells, 0), long_step, 0)
    for part in range(deal):
        lot(0, part, out1, in1).wait_recv()
        hub(part)
        launch(1, part, out2, in2)
        in2[me * deal + part] = out2[me * deal + part]
        if part < deal - 1:
            lax.fori_loop(*share(long_cells, part + 1), long_step, 0)

    key_at = lax.broadcasted_iota(jnp.int32, (cell, crow), 0)
    query_at = lax.broadcasted_iota(jnp.int32, (cell, crow), 1) // heads
    causal = key_at <= query_at
    query_row = query_at[0:1, :]
    moved_at = jnp.where(key_at < PARTS, key_at * part_rows, key_at)
    moved_at = jnp.where(key_at % part_rows == 0, -1, moved_at)

    def own_block(c):
        rows = rows_of(c, crow)
        low = jnp.where(query_row < bound[c], 0, bound[c])
        scores = jnp.where(causal & (key_at >= low), dot(k_ref[c], q_ref[rows, :], NT), NEG)
        return scores, dot(v_ref[c], g_ref[rows, :], NT)

    def own_stats(c, _):
        scores, prob_grad = own_block(c)
        top = jnp.max(scores, axis=0, keepdims=True)
        unnorm = jnp.exp2((scores - top) * (scale * LOG2E))
        stats[c, 0:1] = top
        stats[c, 1:2] = jnp.sum(unnorm, axis=0, keepdims=True)
        stats[c, 2:3] = jnp.sum(unnorm * prob_grad, axis=0, keepdims=True)
        return 0

    lax.fori_loop(0, cells, own_stats, 0, unroll=4)

    sent(0, out1, in1)
    for part in range(deal):
        lot(1, part, out2, in2).wait_recv()
    swaps = []
    for part in range(CHUNKS):
        span = pl.ds(part * chunk, chunk)
        for c in range(part * chunk, (part + 1) * chunk):
            took = in2[pl.ds(jnp.maximum(slot[c], 0) * PARTS, PARTS)]
            prev[core, c] = took.reshape(cell, width)
        swaps.append(swap(part, prev.at[core, span], prev.at[core, span]))
        swaps[-1].start()

    def cross(c, _):
        rows = rows_of(c, crow)
        quer, grad = q_ref[rows, :], g_ref[rows, :]
        prev_key = prev[0, c]
        mark = prev_key.astype(F32)[0:1, :]
        mark = jnp.concatenate([mark] * (crow // width), axis=1)
        mark = jnp.where(mark > 0.0, mark.astype(jnp.int32), cell)
        low = jnp.where(query_row < bound[c], mark, cell)
        scores = jnp.where(moved_at >= low, dot(prev_key, quer, NT), NEG)
        prob_grad = dot(prev[1, c], grad, NT)
        own_top = stats[c, 0:1]
        top = jnp.maximum(jnp.max(scores, axis=0, keepdims=True), own_top)
        unnorm = jnp.exp2((scores - top) * (scale * LOG2E))
        shrink = jnp.exp2((own_top - top) * (scale * LOG2E))
        inv = 1.0 / (jnp.sum(unnorm, axis=0, keepdims=True) + shrink * stats[c, 1:2])
        delta = inv * (
            jnp.sum(unnorm * prob_grad, axis=0, keepdims=True) + shrink * stats[c, 2:3]
        )
        probs = unnorm * inv
        dscore = (probs * (prob_grad - delta)).astype(BF16)
        stats[c, 0:1] = top
        stats[c, 1:2] = inv
        stats[c, 2:3] = delta
        dscore_prev[c] = dscore
        dprev[0, c] = (dot(dscore, quer) * scale).astype(BF16)
        dprev[1, c] = dot(probs.astype(BF16), grad).astype(BF16)
        return 0

    back = []
    for part in range(CHUNKS):
        span = pl.ds(part * chunk, chunk)
        swaps[part].wait_recv()
        lax.fori_loop(part * chunk, (part + 1) * chunk, cross, 0, unroll=True)
        back.append(swap(CHUNKS + part, dprev.at[sib, span], dprev_rx.at[span]))
        back[-1].start()
    for part in range(CHUNKS):
        back[part].wait_recv()

    def fill3(j, _):
        pos = jnp.maximum(inverse[j], 0)
        block = (dprev[core, pos].astype(F32) + dprev_rx[pos].astype(F32)).astype(BF16)
        out3[pl.ds(j * PARTS, PARTS)] = block.reshape(PARTS, part_rows, width)
        return 0

    lax.fori_loop(0, n_slots, fill3, 0, unroll=2)

    for part in range(deal):
        launch(2, part, out3, in3)
    in3[pl.ds(me * deal, deal)] = mine(out3)
    sent(1, out2, in2)

    def own_grads(c, _):
        rows = rows_of(c, crow)
        quer, grad = q_ref[rows, :], g_ref[rows, :]
        scores, prob_grad = own_block(c)
        probs = jnp.exp2((scores - stats[c, 0:1]) * (scale * LOG2E)) * stats[c, 1:2]
        dscore = (probs * (prob_grad - stats[c, 2:3])).astype(BF16)
        dv = dot(probs.astype(BF16), grad)
        dk = dot(dscore, quer) * scale
        dq = (dot(dscore, k_ref[c], TN) + dot(dscore_prev[c], prev[0, c], TN)) * scale
        kept = plan[c] < 0
        dq_ref[rows, :] = jnp.where(kept, dq_ref[rows, :].astype(F32), dq).astype(BF16)
        own[0, c] = jnp.where(kept, own[0, c], dk)
        own[1, c] = jnp.where(kept, own[1, c], dv)
        return 0

    def hub_back(part):
        def step(k, later):
            at = (n - 1 - k) * deal + part
            out4[at] = later.astype(BF16)
            marks = in1[at].astype(F32)
            return jnp.where(marks[0:1, :] > 0.0, in3[at].astype(F32), later)

        lax.fori_loop(0, n, step, jnp.zeros((part_rows, width), F32), unroll=8)

    lax.fori_loop(*share(cells, 0), own_grads, 0, unroll=2)
    for part in range(deal):
        lot(2, part, out3, in3).wait_recv()
        hub_back(part)
        launch(3, part, out4, in4)
        in4[me * deal + part] = out4[me * deal + part]
        if part < deal - 1:
            lax.fori_loop(*share(cells, part + 1), own_grads, 0, unroll=2)
    swap_own = swap(2 * CHUNKS, own.at[sib], own_rx)
    swap_own.start()
    store_q = pltpu.make_async_copy(dq_ref, dq_hbm, store_sem.at[CHUNKS])
    store_q.start()
    sent(2, out3, in3)
    told.wait_send()
    for part in range(CHUNKS):
        swaps[part].wait_send()
        back[part].wait_send()
    swap_own.wait()
    store_q.wait()
    for part in range(deal):
        lot(3, part, out4, in4).wait_recv()

    def give(part):
        span = pl.ds(part * chunk, chunk)
        where = dkv_hbm.at[core, span]
        return (
            pltpu.make_async_copy(total_ref.at[span], where, store_sem.at[part]),
            swap(2 * CHUNKS + 1 + part, total_ref.at[span], where),
        )

    for part in range(CHUNKS):
        for c in range(part * chunk, (part + 1) * chunk):
            came = in4[pl.ds(jnp.maximum(slot[c], 0) * PARTS, PARTS)].astype(F32).reshape(cell, width)
            back_rows = jnp.where(row_at < PARTS, 0.0, came)
            for i in range(1, PARTS):
                back_rows = jnp.where(row_at == i * part_rows, came[i : i + 1, :], back_rows)
            total = own[core, c] + own_rx[c] + jnp.where(slot[c] >= 0, back_rows, 0.0)
            total_ref[c] = total.astype(BF16)

        for copy in give(part):
            copy.start()

    sent(3, out4, in4)
    for part in range(CHUNKS):
        for copy in give(part):
            copy.wait()


def pin(x):
    return pltpu.with_memory_space_constraint(x, pltpu.HBM)


def on_device(n, query_heads, key_heads, value_heads, attend_grad, doc_ids, cell_plan):
    tokens, _, heads, width = query_heads.shape
    cells = cell_plan.shape[0]
    cell = tokens // cells
    crow = cell * heads

    n_slots = 3 * n // 4
    slots = pltpu.VMEM((n_slots * PARTS, cell // PARTS, width), BF16)
    pair = pltpu.VMEM((2, cells, cell, width), BF16)
    hbm = pl.BlockSpec(memory_space=pl.ANY)
    wide = pltpu.VMEM((tokens * heads, width), BF16)
    narrow = pltpu.VMEM((cells, cell, width), BF16)
    n_swaps = 3 * CHUNKS + 1
    dq, dkv = pl.pallas_call(
        functools.partial(kernel, n, cells, cell, LONG, heads),
        out_shape=(
            jax.ShapeDtypeStruct((tokens * heads, width), BF16),
            jax.ShapeDtypeStruct((2, cells, cell, width), BF16),
        ),
        in_specs=[hbm] * 6,
        out_specs=[hbm] * 2,
        scratch_shapes=[
            pltpu.SMEM((cells,), jnp.int32),
            pltpu.SMEM((tokens,), jnp.int32),
            pltpu.SMEM((n, 8), jnp.int32),
            pltpu.SMEM((n,), jnp.int32),
            pltpu.SMEM((cells,), jnp.int32),
            pltpu.SMEM((n_slots,), jnp.int32),
            pltpu.SMEM((cells,), jnp.int32),
            wide, narrow, narrow, wide, wide, narrow, narrow,
        ]
        + [slots] * 8
        + [
            pair, pair, narrow,
            pltpu.VMEM((2, cells, cell, width), F32),
            pltpu.VMEM((cells, cell, width), F32),
            pltpu.VMEM((cells, 8, crow), F32),
            pltpu.VMEM((cells, cell, crow), BF16),
            pltpu.SemaphoreType.DMA((6,)),
            pltpu.SemaphoreType.DMA((2,)),
            pltpu.SemaphoreType.DMA((4, n_slots * PARTS // n)),
            pltpu.SemaphoreType.DMA((4, n_slots * PARTS // n)),
            pltpu.SemaphoreType.DMA((n_swaps,)),
            pltpu.SemaphoreType.DMA((n_swaps,)),
            pltpu.SemaphoreType.DMA((CHUNKS + 1,)),
        ],
        compiler_params=pltpu.CompilerParams(
            collective_id=0, has_side_effects=True, vmem_limit_bytes=48 * 2**20
        ),
    )(
        pin(cell_plan),
        pin(doc_ids),
        pin(query_heads.reshape(tokens * heads, width)),
        pin(key_heads.reshape(cells, cell, width)),
        pin(value_heads.reshape(cells, cell, width)),
        pin(attend_grad.reshape(tokens * heads, width)),
    )
    return (
        dq.reshape(tokens, 1, heads, width),
        dkv[0].reshape(tokens, 1, width),
        dkv[1].reshape(tokens, 1, width),
    )


def solution(mesh):
    wide = P("dp", "tensor", "section", None)
    narrow = P("dp", "tensor", None)
    return jax.shard_map(
        functools.partial(on_device, mesh.shape["dp"]),
        mesh=mesh,
        in_specs=(wide, narrow, narrow, wide, P("dp"), P("dp")),
        out_specs=(wide, narrow, narrow),
        check_vma=False,
    )
```

```python
import functools

import jax
import jax.numpy as jnp
from jax import lax
from jax.experimental import pallas as pl
from jax.experimental.pallas import tpu as pltpu
from jax.sharding import PartitionSpec as P

LONG = 8
CHUNKS = 4
PARTS = 4
RING = 8
MESH = pl.DeviceIdType.MESH
LOG2E = 1.4426950408889634
NEG = -1e30
F32 = jnp.float32
BF16 = jnp.bfloat16
NT = (((1,), (1,)), ((), ()))
TN = (((0,), (0,)), ((), ()))


def dot(a, b, dims=(((1,), (0,)), ((), ()))):
    return lax.dot_general(a, b, dims, preferred_element_type=F32)


def softmax_grads(keys, vals, quer, grad, mask, scale):
    scores = jnp.where(mask, dot(keys, quer, NT), NEG)
    prob_grad = dot(vals, grad, NT)
    top = jnp.max(scores, axis=0, keepdims=True)
    unnorm = jnp.exp2((scores - top) * (scale * LOG2E))
    probs = unnorm * (1.0 / jnp.sum(unnorm, axis=0, keepdims=True))
    delta = jnp.sum(probs * prob_grad, axis=0, keepdims=True)
    dscore = (probs * (prob_grad - delta)).astype(BF16)
    dv = dot(probs.astype(BF16), grad)
    dk = dot(dscore, quer) * scale
    dq = dot(dscore, keys, TN) * scale
    return dq, dk, dv


def kernel(
    n, cells, cell, long_cells, heads,
    plan_hbm, doc_hbm, q_hbm, k_hbm, v_hbm, g_hbm,
    dq_hbm, dkv_hbm,
    plan, doc, flags, rank, slot, inverse, bound, q_ref, k_ref, v_ref, g_ref, dq_ref, total_ref, marked,
    in1, out1, out2, in3, out3, in4, out4,
    prev, dprev, dprev_rx, own, own_rx, stats, final, dscores,
    load_sem, flag_sem, send_sem, recv_sem, sib_send, sib_recv, store_sem,
):
    me = lax.axis_index("dp")
    core = lax.axis_index("section")
    sib = 1 - core
    crow = cell * heads
    width = q_ref.shape[-1]
    scale = width ** -0.5
    chunk = cells // CHUNKS
    part_rows = cell // PARTS
    n_slots = 3 * n // 4
    turns = n_slots * PARTS // n
    per_turn = n_slots // turns
    ring = min(RING, n)
    lines = n // ring
    line_at, ring_at = me // ring, lax.rem(me, ring)

    def peer_of(k):
        turn = k // lines
        odd = lax.rem(turn, 2)
        offset = ring // 2 + odd * (turn + 1) // 2 - (1 - odd) * (turn // 2)
        line = lax.rem(line_at + lines - 1 - lax.rem(k, lines), lines)
        return line * ring + lax.rem(ring_at + offset, ring)

    def each_peer(act):
        def step(k, _):
            act(peer_of(k))
            return 0

        lax.fori_loop(0, n - 1, step, 0, unroll=True)

    loads = [
        pltpu.make_async_copy(src, dst, load_sem.at[i])
        for i, (src, dst) in enumerate(
            ((plan_hbm, plan), (doc_hbm, doc), (k_hbm, k_ref), (v_hbm, v_ref), (q_hbm, q_ref), (g_hbm, g_ref))
        )
    ]
    for load in loads:
        load.start()

    barrier = pltpu.get_barrier_semaphore()

    def greet(peer):
        pl.semaphore_signal(barrier, inc=1, device_id={"dp": peer}, device_id_type=MESH)

    each_peer(greet)
    pl.semaphore_signal(barrier, inc=1, device_id={"section": sib}, device_id_type=MESH)

    def launch(phase, turn, src, dst):
        def send(peer):
            pltpu.make_async_remote_copy(
                src_ref=src.at[turn * n + peer],
                dst_ref=dst.at[turn * n + me],
                send_sem=send_sem.at[phase, turn],
                recv_sem=recv_sem.at[phase, turn],
                device_id={"dp": peer},
                device_id_type=MESH,
            ).start()

        dst[turn * n + me] = src[turn * n + me]
        each_peer(send)

    def lot(phase, turn, src, dst):
        return pltpu.make_async_remote_copy(
            src_ref=src.at[pl.ds(0, n - 1)],
            dst_ref=dst.at[pl.ds(0, n - 1)],
            send_sem=send_sem.at[phase, turn],
            recv_sem=recv_sem.at[phase, turn],
            device_id={"section": sib},
            device_id_type=MESH,
        )

    def sent(phase, src, dst):
        for turn in range(turns):
            lot(phase, turn, src, dst).wait_send()

    def swap(which, src, dst):
        return pltpu.make_async_remote_copy(
            src_ref=src,
            dst_ref=dst,
            send_sem=sib_send.at[which],
            recv_sem=sib_recv.at[which],
            device_id={"section": sib},
            device_id_type=MESH,
        )

    loads[0].wait()
    loads[1].wait()

    def bounds(c, _):
        base = c * cell
        lead = doc[base]
        last = jnp.int32(0)
        step = cell // 2
        while step:
            last = jnp.where(doc[base + last + step] == lead, last + step, last)
            step //= 2
        bound[c] = last + 1
        return 0

    lax.fori_loop(0, cells, bounds, 0, unroll=4)

    for i in range(flags.shape[1]):
        flags[me, i] = plan[0]

    loads[2].wait()
    loads[3].wait()
    row_at = lax.broadcasted_iota(jnp.int32, (cell, width), 0)

    def mark(c, _):
        block = jnp.where(core == 0, k_ref[c], v_ref[c]).astype(F32)
        moved = block
        for i in range(1, PARTS):
            moved = jnp.where(row_at == i, block[i * part_rows : i * part_rows + 1, :], moved)
        moved = jnp.where(row_at % part_rows == 0, bound[c].astype(F32), moved)
        marked[c] = moved.astype(BF16)
        return 0

    lax.fori_loop(0, cells, mark, 0, unroll=4)

    pl.semaphore_wait(barrier, n)

    def tell(peer):
        pltpu.make_async_remote_copy(
            src_ref=flags.at[me],
            dst_ref=flags.at[me],
            send_sem=flag_sem.at[0],
            recv_sem=flag_sem.at[1],
            device_id={"dp": peer},
            device_id_type=MESH,
        ).start()

    each_peer(tell)
    told = pltpu.make_async_remote_copy(
        src_ref=flags.at[pl.ds(0, n - 1)],
        dst_ref=flags.at[pl.ds(0, n - 1)],
        send_sem=flag_sem.at[0],
        recv_sem=flag_sem.at[1],
        device_id={"section": sib},
        device_id_type=MESH,
    )
    loads[4].wait()
    loads[5].wait()
    long_len = long_cells * cell
    own[:, long_cells:] = jnp.zeros((2, cells - long_cells, cell, width), F32)
    dq_ref[long_cells:] = jnp.zeros((cells - long_cells, crow, width), BF16)
    long_key = lax.broadcasted_iota(jnp.int32, (long_len, crow), 0)
    long_query = lax.broadcasted_iota(jnp.int32, (long_len, crow), 1) // heads

    def long_step(c):
        seen = min(2 * (c // 2) + 2, long_cells)
        flat = (seen * cell, width)
        dq, dk, dv = softmax_grads(
            k_ref[:seen].reshape(flat), v_ref[:seen].reshape(flat), q_ref[c], g_ref[c],
            long_key[: seen * cell] <= long_query[: seen * cell] + c * cell, scale,
        )
        dq_ref[c] = dq.astype(BF16)
        for which, grads in ((0, dk), (1, dv)):
            grads = grads.reshape(seen, cell, width)
            if c == long_cells - 1:
                own[which, :seen] = grads
            else:
                own[which, :seen] += grads

    key_at = lax.broadcasted_iota(jnp.int32, (cell, crow), 0)
    query_at = lax.broadcasted_iota(jnp.int32, (cell, crow), 1) // heads
    causal = key_at <= query_at
    query_row = query_at[0:1, :]
    moved_at = jnp.where(key_at < PARTS, key_at * part_rows, key_at)
    moved_at = jnp.where(key_at % part_rows == 0, -1, moved_at)

    def own_block(c):
        low = jnp.where(query_row < bound[c], 0, bound[c])
        scores = jnp.where(causal & (key_at >= low), dot(k_ref[c], q_ref[c], NT), NEG)
        return scores, dot(v_ref[c], g_ref[c], NT)

    def own_stats(c, _):
        scores, prob_grad = own_block(c)
        top = jnp.max(scores, axis=0, keepdims=True)
        unnorm = jnp.exp2((scores - top) * (scale * LOG2E))
        stats[c, 0:1] = top
        stats[c, 1:2] = jnp.sum(unnorm, axis=0, keepdims=True)
        stats[c, 2:3] = jnp.sum(unnorm * prob_grad, axis=0, keepdims=True)
        return 0

    lax.fori_loop(0, cells, own_stats, 0, unroll=4)

    for c in range(long_cells - 1, long_cells - 2, -1):
        long_step(c)
    told.wait_recv()

    keepers = jnp.int32(0)
    for d in range(n):
        rank[d] = d - keepers
        keepers += jnp.where(flags[d, 0] < 0, 1, 0)
    for c in range(cells):
        slot[c] = jnp.where(plan[c] >= 0, rank[jnp.maximum(plan[c], 0)], -1)

    def fill(j, _):
        at = jnp.int32(-1)
        for c in range(cells):
            at = jnp.where(slot[c] == j, c, at)
        inverse[j] = at
        block = jnp.where(at >= 0, marked[jnp.maximum(at, 0)], jnp.zeros((cell, width), BF16))
        out1[pl.ds(j * PARTS, PARTS)] = block.reshape(PARTS, part_rows, width)
        return 0

    lax.fori_loop(0, n_slots, fill, 0, unroll=2)

    for turn in range(turns):
        launch(0, turn, out1, in1)
    for c in range(long_cells - 2, 3, -1):
        long_step(c)

    def hub(turn):
        def step(r, last):
            at = turn * n + r
            out2[at] = last.astype(BF16)
            block = in1[at].astype(F32)
            return jnp.where(block[0:1, :] > 0.0, block, last)

        lax.fori_loop(0, n, step, jnp.zeros((part_rows, width), F32), unroll=8)

    mine = prev.at[core]
    for turn in range(turns):
        lot(0, turn, out1, in1).wait_recv()
        hub(turn)
        launch(1, turn, out2, mine)

    def swap_prev(turn):
        span = pl.ds(turn * n, n)
        return swap(turn, prev.at[core, span], prev.at[core, span])

    def slot_rows(j):
        return pl.ds(j * PARTS, PARTS)

    def cross(j):
        c = jnp.maximum(inverse[j], 0)
        quer, grad = q_ref[c], g_ref[c]
        prev_key = prev[0, slot_rows(j)].reshape(cell, width)
        mark = prev_key.astype(F32)[0:1, :]
        mark = jnp.concatenate([mark] * (crow // width), axis=1)
        mark = jnp.where(mark > 0.0, mark.astype(jnp.int32), cell)
        low = jnp.where(query_row < bound[c], mark, cell)
        scores = jnp.where(moved_at >= low, dot(prev_key, quer, NT), NEG)
        prob_grad = dot(prev[1, slot_rows(j)].reshape(cell, width), grad, NT)
        own_top = stats[c, 0:1]
        top = jnp.maximum(jnp.max(scores, axis=0, keepdims=True), own_top)
        unnorm = jnp.exp2((scores - top) * (scale * LOG2E))
        shrink = jnp.exp2((own_top - top) * (scale * LOG2E))
        inv = 1.0 / (jnp.sum(unnorm, axis=0, keepdims=True) + shrink * stats[c, 1:2])
        delta = inv * (
            jnp.sum(unnorm * prob_grad, axis=0, keepdims=True) + shrink * stats[c, 2:3]
        )
        probs = unnorm * inv
        dscore = (probs * (prob_grad - delta)).astype(BF16)
        final[j, 0:1] = top
        final[j, 1:2] = inv
        final[j, 2:3] = delta
        dscores[j] = dscore
        shape = (PARTS, part_rows, width)
        dprev[0, slot_rows(j)] = (dot(dscore, quer) * scale).astype(BF16).reshape(shape)
        dprev[1, slot_rows(j)] = dot(probs.astype(BF16), grad).astype(BF16).reshape(shape)

    def swap_back(turn):
        span = pl.ds(turn * n, n)
        return swap(turns + turn, dprev.at[sib, span], dprev_rx.at[span])

    def attend(turn):
        swap_prev(turn).wait_recv()
        for j in range(turn * per_turn, (turn + 1) * per_turn):
            cross(j)
        swap_back(turn).start()

    def give_back(turn):
        swap_back(turn).wait_recv()
        span = pl.ds(turn * n, n)
        out3[span] = (dprev[core, span].astype(F32) + dprev_rx[span].astype(F32)).astype(BF16)
        launch(2, turn, out3, in3)

    def own_grads(c, _):
        j = jnp.maximum(slot[c], 0)
        quer, grad = q_ref[c], g_ref[c]
        scores, prob_grad = own_block(c)
        probs = jnp.exp2((scores - final[j, 0:1]) * (scale * LOG2E)) * final[j, 1:2]
        dscore = (probs * (prob_grad - final[j, 2:3])).astype(BF16)
        dv = dot(probs.astype(BF16), grad)
        dk = dot(dscore, quer) * scale
        both = jnp.concatenate([dscores[j], dscore], axis=0)
        keys = jnp.concatenate([prev[0, slot_rows(j)].reshape(cell, width), k_ref[c]], axis=0)
        dq = dot(both, keys, TN) * scale
        kept = plan[c] < 0
        dq_ref[c] = jnp.where(kept, dq_ref[c].astype(F32), dq).astype(BF16)
        own[0, c] = jnp.where(kept, own[0, c], dk)
        own[1, c] = jnp.where(kept, own[1, c], dv)
        return 0

    def hub_back(turn):
        def step(k, later):
            at = turn * n + n - 1 - k
            out4[at] = later.astype(BF16)
            marks = in1[at].astype(F32)
            return jnp.where(marks[0:1, :] > 0.0, in3[at].astype(F32), later)

        lax.fori_loop(0, n, step, jnp.zeros((part_rows, width), F32), unroll=8)

    def pass_back(turn):
        lot(2, turn, out3, in3).wait_recv()
        hub_back(turn)
        launch(3, turn, out4, in4)

    def arrive(turn):
        lot(1, turn, out2, mine).wait_recv()
        swap_prev(turn).start()

    arrive(0)
    for turn in range(turns):
        if turn + 1 < turns:
            arrive(turn + 1)
        attend(turn)
        if turn:
            give_back(turn - 1)
    for c in range(3, -1, -1):
        long_step(c)
    give_back(turns - 1)
    for turn in range(turns):
        pass_back(turn)
        if turn + 1 < turns:
            lax.fori_loop(4 * turn, 4 * turn + 4, own_grads, 0, unroll=4)
    lax.fori_loop(4 * (turns - 1), cells, own_grads, 0, unroll=4)
    swap_own = swap(2 * turns, own.at[sib], own_rx)
    swap_own.start()
    store_q = pltpu.make_async_copy(dq_ref, dq_hbm, store_sem.at[CHUNKS])
    store_q.start()
    sent(0, out1, in1)
    sent(1, out2, mine)
    sent(2, out3, in3)
    told.wait_send()
    for turn in range(turns):
        swap_prev(turn).wait_send()
        swap_back(turn).wait_send()
    swap_own.wait()
    store_q.wait()
    for turn in range(turns):
        lot(3, turn, out4, in4).wait_recv()

    def give(part):
        span = pl.ds(part * chunk, chunk)
        where = dkv_hbm.at[core, span]
        return (
            pltpu.make_async_copy(total_ref.at[span], where, store_sem.at[part]),
            swap(2 * turns + 1 + part, total_ref.at[span], where),
        )

    for part in range(CHUNKS):
        for i in range(chunk):
            c = part * chunk + i
            came = in4[pl.ds(jnp.maximum(slot[c], 0) * PARTS, PARTS)].astype(F32).reshape(cell, width)
            back_rows = jnp.where(row_at < PARTS, 0.0, came)
            for j in range(1, PARTS):
                back_rows = jnp.where(row_at == j * part_rows, came[j : j + 1, :], back_rows)
            total = own[core, c] + own_rx[c] + jnp.where(slot[c] >= 0, back_rows, 0.0)
            total_ref[c] = total.astype(BF16)
        for copy in give(part):
            copy.start()

    sent(3, out4, in4)
    for part in range(CHUNKS):
        for copy in give(part):
            copy.wait()


def pin(x):
    return pltpu.with_memory_space_constraint(x, pltpu.HBM)


def on_device(n, query_heads, key_heads, value_heads, attend_grad, doc_ids, cell_plan):
    tokens, _, heads, width = query_heads.shape
    cells = cell_plan.shape[0]
    cell = tokens // cells
    crow = cell * heads

    n_slots = 3 * n // 4
    slots = pltpu.VMEM((n_slots * PARTS, cell // PARTS, width), BF16)
    both = pltpu.VMEM((2, n_slots * PARTS, cell // PARTS, width), BF16)
    hbm = pl.BlockSpec(memory_space=pl.ANY)
    wide = pltpu.VMEM((cells, crow, width), BF16)
    narrow = pltpu.VMEM((cells, cell, width), BF16)
    n_swaps = 2 * (n_slots * PARTS // n) + 1 + CHUNKS
    dq, dkv = pl.pallas_call(
        functools.partial(kernel, n, cells, cell, LONG, heads),
        out_shape=(
            jax.ShapeDtypeStruct((cells, crow, width), BF16),
            jax.ShapeDtypeStruct((2, cells, cell, width), BF16),
        ),
        in_specs=[hbm] * 6,
        out_specs=[hbm] * 2,
        scratch_shapes=[
            pltpu.SMEM((cells,), jnp.int32),
            pltpu.SMEM((tokens,), jnp.int32),
            pltpu.SMEM((n, 8), jnp.int32),
            pltpu.SMEM((n,), jnp.int32),
            pltpu.SMEM((cells,), jnp.int32),
            pltpu.SMEM((n_slots,), jnp.int32),
            pltpu.SMEM((cells,), jnp.int32),
            wide, narrow, narrow, wide, wide, narrow, narrow,
        ]
        + [slots] * 7
        + [
            both, both, slots,
            pltpu.VMEM((2, cells, cell, width), F32),
            pltpu.VMEM((cells, cell, width), F32),
            pltpu.VMEM((cells, 8, crow), F32),
            pltpu.VMEM((n_slots, 8, crow), F32),
            pltpu.VMEM((n_slots, cell, crow), BF16),
            pltpu.SemaphoreType.DMA((6,)),
            pltpu.SemaphoreType.DMA((2,)),
            pltpu.SemaphoreType.DMA((4, n_slots * PARTS // n)),
            pltpu.SemaphoreType.DMA((4, n_slots * PARTS // n)),
            pltpu.SemaphoreType.DMA((n_swaps,)),
            pltpu.SemaphoreType.DMA((n_swaps,)),
            pltpu.SemaphoreType.DMA((CHUNKS + 1,)),
        ],
        compiler_params=pltpu.CompilerParams(
            collective_id=0, has_side_effects=True, vmem_limit_bytes=48 * 2**20
        ),
    )(
        pin(cell_plan),
        pin(doc_ids),
        pin(query_heads.reshape(cells, crow, width)),
        pin(key_heads.reshape(cells, cell, width)),
        pin(value_heads.reshape(cells, cell, width)),
        pin(attend_grad.reshape(cells, crow, width)),
    )
    return (
        dq.reshape(tokens, 1, heads, width),
        dkv[0].reshape(tokens, 1, width),
        dkv[1].reshape(tokens, 1, width),
    )


def solution(mesh):
    wide = P("dp", "tensor", "section", None)
    narrow = P("dp", "tensor", None)
    return jax.shard_map(
        functools.partial(on_device, mesh.shape["dp"]),
        mesh=mesh,
        in_specs=(wide, narrow, narrow, wide, P("dp"), P("dp")),
        out_specs=(wide, narrow, narrow),
        check_vma=False,
    )
```

```python
import functools

import jax
import jax.numpy as jnp
from jax import lax
from jax.experimental import pallas as pl
from jax.experimental.pallas import tpu as pltpu
from jax.sharding import PartitionSpec as P

LONG = 8
CHUNKS = 4
PARTS = 4
RING = 8
MESH = pl.DeviceIdType.MESH
LOG2E = 1.4426950408889634
NEG = -1e30
F32 = jnp.float32
BF16 = jnp.bfloat16
NT = (((1,), (1,)), ((), ()))
TN = (((0,), (0,)), ((), ()))


def dot(a, b, dims=(((1,), (0,)), ((), ()))):
    return lax.dot_general(a, b, dims, preferred_element_type=F32)


def softmax_grads(keys, vals, quer, grad, mask, scale):
    scores = jnp.where(mask, dot(keys, quer, NT), NEG)
    prob_grad = dot(vals, grad, NT)
    top = jnp.max(scores, axis=0, keepdims=True)
    unnorm = jnp.exp2((scores - top) * (scale * LOG2E))
    probs = unnorm * (1.0 / jnp.sum(unnorm, axis=0, keepdims=True))
    delta = jnp.sum(probs * prob_grad, axis=0, keepdims=True)
    dscore = (probs * (prob_grad - delta)).astype(BF16)
    dv = dot(probs.astype(BF16), grad)
    dk = dot(dscore, quer) * scale
    dq = dot(dscore, keys, TN) * scale
    return dq, dk, dv


def kernel(
    n, cells, cell, long_cells, heads,
    plan_hbm, doc_hbm, q_hbm, k_hbm, v_hbm, g_hbm,
    dq_hbm, dkv_hbm,
    plan, doc, flags, rank, slot, inverse, bound, q_ref, k_ref, v_ref, g_ref, dq_ref, total_ref, marked,
    in1, out1, out2, in3, out3, in4, out4,
    prev, dprev, dprev_rx, own, own_rx, stats, final, dscores,
    load_sem, flag_sem, send_sem, recv_sem, sib_send, sib_recv, store_sem,
):
    me = lax.axis_index("dp")
    core = lax.axis_index("section")
    sib = 1 - core
    crow = cell * heads
    width = q_ref.shape[-1]
    scale = width ** -0.5
    chunk = cells // CHUNKS
    part_rows = cell // PARTS
    n_slots = 3 * n // 4
    turns = n_slots * PARTS // n
    per_turn = n_slots // turns
    ring = min(RING, n)
    lines = n // ring
    line_at, ring_at = me // ring, lax.rem(me, ring)

    def peer_of(k):
        turn = k // lines
        odd = lax.rem(turn, 2)
        offset = ring // 2 + odd * (turn + 1) // 2 - (1 - odd) * (turn // 2)
        line = lax.rem(line_at + lines - 1 - lax.rem(k, lines), lines)
        return line * ring + lax.rem(ring_at + offset, ring)

    def each_peer(act):
        def step(k, _):
            act(peer_of(k))
            return 0

        lax.fori_loop(0, n - 1, step, 0, unroll=True)

    barrier = pltpu.get_barrier_semaphore()

    def greet(peer):
        pl.semaphore_signal(barrier, inc=1, device_id={"dp": peer}, device_id_type=MESH)

    each_peer(greet)
    pl.semaphore_signal(barrier, inc=1, device_id={"section": sib}, device_id_type=MESH)

    loads = [
        pltpu.make_async_copy(src, dst, load_sem.at[i])
        for i, (src, dst) in enumerate(
            ((plan_hbm, plan), (doc_hbm, doc), (k_hbm, k_ref), (v_hbm, v_ref), (q_hbm, q_ref), (g_hbm, g_ref))
        )
    ]
    for load in loads:
        load.start()

    def launch(phase, turn, src, dst):
        def send(peer):
            pltpu.make_async_remote_copy(
                src_ref=src.at[turn * n + peer],
                dst_ref=dst.at[turn * n + me],
                send_sem=send_sem.at[phase, turn],
                recv_sem=recv_sem.at[phase, turn],
                device_id={"dp": peer},
                device_id_type=MESH,
            ).start()

        dst[turn * n + me] = src[turn * n + me]
        each_peer(send)

    def lot(phase, turn, src, dst):
        return pltpu.make_async_remote_copy(
            src_ref=src.at[pl.ds(0, n - 1)],
            dst_ref=dst.at[pl.ds(0, n - 1)],
            send_sem=send_sem.at[phase, turn],
            recv_sem=recv_sem.at[phase, turn],
            device_id={"section": sib},
            device_id_type=MESH,
        )

    def sent(phase, src, dst):
        for turn in range(turns):
            lot(phase, turn, src, dst).wait_send()

    def swap(which, src, dst):
        return pltpu.make_async_remote_copy(
            src_ref=src,
            dst_ref=dst,
            send_sem=sib_send.at[which],
            recv_sem=sib_recv.at[which],
            device_id={"section": sib},
            device_id_type=MESH,
        )

    loads[0].wait()
    for i in range(flags.shape[1]):
        flags[me, i] = plan[0]

    pl.semaphore_wait(barrier, n)

    def tell(peer):
        pltpu.make_async_remote_copy(
            src_ref=flags.at[me],
            dst_ref=flags.at[me],
            send_sem=flag_sem.at[0],
            recv_sem=flag_sem.at[1],
            device_id={"dp": peer},
            device_id_type=MESH,
        ).start()

    each_peer(tell)
    told = pltpu.make_async_remote_copy(
        src_ref=flags.at[pl.ds(0, n - 1)],
        dst_ref=flags.at[pl.ds(0, n - 1)],
        send_sem=flag_sem.at[0],
        recv_sem=flag_sem.at[1],
        device_id={"section": sib},
        device_id_type=MESH,
    )

    loads[1].wait()

    def bounds(c, _):
        base = c * cell
        lead = doc[base]
        last = jnp.int32(0)
        step = cell // 2
        while step:
            last = jnp.where(doc[base + last + step] == lead, last + step, last)
            step //= 2
        bound[c] = last + 1
        return 0

    lax.fori_loop(0, cells, bounds, 0, unroll=4)

    loads[2].wait()
    loads[3].wait()
    row_at = lax.broadcasted_iota(jnp.int32, (cell, width), 0)

    def mark(c, _):
        block = jnp.where(core == 0, k_ref[c], v_ref[c]).astype(F32)
        moved = block
        for i in range(1, PARTS):
            moved = jnp.where(row_at == i, block[i * part_rows : i * part_rows + 1, :], moved)
        moved = jnp.where(row_at % part_rows == 0, bound[c].astype(F32), moved)
        marked[c] = moved.astype(BF16)
        return 0

    lax.fori_loop(0, cells, mark, 0, unroll=4)

    loads[4].wait()
    loads[5].wait()
    long_len = long_cells * cell
    own[:, long_cells:] = jnp.zeros((2, cells - long_cells, cell, width), F32)
    dq_ref[long_cells:] = jnp.zeros((cells - long_cells, crow, width), BF16)
    long_key = lax.broadcasted_iota(jnp.int32, (long_len, crow), 0)
    long_query = lax.broadcasted_iota(jnp.int32, (long_len, crow), 1) // heads

    def long_step(c):
        seen = min(2 * (c // 2) + 2, long_cells)
        flat = (seen * cell, width)
        dq, dk, dv = softmax_grads(
            k_ref[:seen].reshape(flat), v_ref[:seen].reshape(flat), q_ref[c], g_ref[c],
            long_key[: seen * cell] <= long_query[: seen * cell] + c * cell, scale,
        )
        dq_ref[c] = dq.astype(BF16)
        for which, grads in ((0, dk), (1, dv)):
            grads = grads.reshape(seen, cell, width)
            if c == long_cells - 1:
                own[which, :seen] = grads
            else:
                own[which, :seen] += grads

    key_at = lax.broadcasted_iota(jnp.int32, (cell, crow), 0)
    query_at = lax.broadcasted_iota(jnp.int32, (cell, crow), 1) // heads
    causal = key_at <= query_at
    query_row = query_at[0:1, :]
    moved_at = jnp.where(key_at < PARTS, key_at * part_rows, key_at)
    moved_at = jnp.where(key_at % part_rows == 0, -1, moved_at)

    def own_block(c):
        low = jnp.where(query_row < bound[c], 0, bound[c])
        scores = jnp.where(causal & (key_at >= low), dot(k_ref[c], q_ref[c], NT), NEG)
        return scores, dot(v_ref[c], g_ref[c], NT)

    def own_stats(c, _):
        scores, prob_grad = own_block(c)
        top = jnp.max(scores, axis=0, keepdims=True)
        unnorm = jnp.exp2((scores - top) * (scale * LOG2E))
        stats[c, 0:1] = top
        stats[c, 1:2] = jnp.sum(unnorm, axis=0, keepdims=True)
        stats[c, 2:3] = jnp.sum(unnorm * prob_grad, axis=0, keepdims=True)
        return 0

    lax.fori_loop(0, cells, own_stats, 0, unroll=4)

    for c in range(long_cells - 1, long_cells - 2, -1):
        long_step(c)
    told.wait_recv()

    keepers = jnp.int32(0)
    for d in range(n):
        rank[d] = d - keepers
        keepers += jnp.where(flags[d, 0] < 0, 1, 0)
    for c in range(cells):
        slot[c] = jnp.where(plan[c] >= 0, rank[jnp.maximum(plan[c], 0)], -1)

    def fill(j, _):
        at = jnp.int32(-1)
        for c in range(cells):
            at = jnp.where(slot[c] == j, c, at)
        inverse[j] = at
        block = jnp.where(at >= 0, marked[jnp.maximum(at, 0)], jnp.zeros((cell, width), BF16))
        out1[pl.ds(j * PARTS, PARTS)] = block.reshape(PARTS, part_rows, width)
        return 0

    lax.fori_loop(0, n_slots, fill, 0, unroll=2)

    for turn in range(turns):
        launch(0, turn, out1, in1)
    for c in range(long_cells - 2, 3, -1):
        long_step(c)

    def hub(turn):
        def step(r, last):
            at = turn * n + r
            out2[at] = last.astype(BF16)
            block = in1[at].astype(F32)
            return jnp.where(block[0:1, :] > 0.0, block, last)

        lax.fori_loop(0, n, step, jnp.zeros((part_rows, width), F32), unroll=8)

    mine = prev.at[core]
    for turn in range(turns):
        lot(0, turn, out1, in1).wait_recv()
        hub(turn)
        launch(1, turn, out2, mine)

    def swap_prev(turn):
        span = pl.ds(turn * n, n)
        return swap(turn, prev.at[core, span], prev.at[core, span])

    def slot_rows(j):
        return pl.ds(j * PARTS, PARTS)

    def cross(j):
        c = jnp.maximum(inverse[j], 0)
        quer, grad = q_ref[c], g_ref[c]
        prev_key = prev[0, slot_rows(j)].reshape(cell, width)
        mark = prev_key.astype(F32)[0:1, :]
        mark = jnp.concatenate([mark] * (crow // width), axis=1)
        mark = jnp.where(mark > 0.0, mark.astype(jnp.int32), cell)
        low = jnp.where(query_row < bound[c], mark, cell)
        scores = jnp.where(moved_at >= low, dot(prev_key, quer, NT), NEG)
        prob_grad = dot(prev[1, slot_rows(j)].reshape(cell, width), grad, NT)
        own_top = stats[c, 0:1]
        top = jnp.maximum(jnp.max(scores, axis=0, keepdims=True), own_top)
        unnorm = jnp.exp2((scores - top) * (scale * LOG2E))
        shrink = jnp.exp2((own_top - top) * (scale * LOG2E))
        inv = 1.0 / (jnp.sum(unnorm, axis=0, keepdims=True) + shrink * stats[c, 1:2])
        delta = inv * (
            jnp.sum(unnorm * prob_grad, axis=0, keepdims=True) + shrink * stats[c, 2:3]
        )
        probs = unnorm * inv
        dscore = (probs * (prob_grad - delta)).astype(BF16)
        final[j, 0:1] = top
        final[j, 1:2] = inv
        final[j, 2:3] = delta
        dscores[j] = dscore
        shape = (PARTS, part_rows, width)
        dprev[0, slot_rows(j)] = (dot(dscore, quer) * scale).astype(BF16).reshape(shape)
        dprev[1, slot_rows(j)] = dot(probs.astype(BF16), grad).astype(BF16).reshape(shape)

    def swap_back(turn):
        span = pl.ds(turn * n, n)
        return swap(turns + turn, dprev.at[sib, span], dprev_rx.at[span])

    def attend(turn):
        swap_prev(turn).wait_recv()
        for j in range(turn * per_turn, (turn + 1) * per_turn):
            cross(j)
        swap_back(turn).start()

    def give_back(turn):
        swap_back(turn).wait_recv()
        span = pl.ds(turn * n, n)
        out3[span] = (dprev[core, span].astype(F32) + dprev_rx[span].astype(F32)).astype(BF16)
        launch(2, turn, out3, in3)

    def own_grads(c, _):
        j = jnp.maximum(slot[c], 0)
        quer, grad = q_ref[c], g_ref[c]
        scores, prob_grad = own_block(c)
        probs = jnp.exp2((scores - final[j, 0:1]) * (scale * LOG2E)) * final[j, 1:2]
        dscore = (probs * (prob_grad - final[j, 2:3])).astype(BF16)
        dv = dot(probs.astype(BF16), grad)
        dk = dot(dscore, quer) * scale
        both = jnp.concatenate([dscores[j], dscore], axis=0)
        keys = jnp.concatenate([prev[0, slot_rows(j)].reshape(cell, width), k_ref[c]], axis=0)
        dq = dot(both, keys, TN) * scale
        kept = plan[c] < 0
        dq_ref[c] = jnp.where(kept, dq_ref[c].astype(F32), dq).astype(BF16)
        own[0, c] = jnp.where(kept, own[0, c], dk)
        own[1, c] = jnp.where(kept, own[1, c], dv)
        return 0

    def hub_back(turn):
        def step(k, later):
            at = turn * n + n - 1 - k
            out4[at] = later.astype(BF16)
            marks = in1[at].astype(F32)
            return jnp.where(marks[0:1, :] > 0.0, in3[at].astype(F32), later)

        lax.fori_loop(0, n, step, jnp.zeros((part_rows, width), F32), unroll=8)

    def pass_back(turn):
        lot(2, turn, out3, in3).wait_recv()
        hub_back(turn)
        launch(3, turn, out4, in4)

    def arrive(turn):
        lot(1, turn, out2, mine).wait_recv()
        swap_prev(turn).start()

    arrive(0)
    attend(0)
    arrive(1)
    give_back(0)
    attend(1)
    arrive(2)
    give_back(1)
    attend(2)
    give_back(2)
    for c in range(3, -1, -1):
        long_step(c)
    pass_back(0)
    lax.fori_loop(0, 4, own_grads, 0, unroll=4)
    pass_back(1)
    lax.fori_loop(4, 8, own_grads, 0, unroll=4)
    pass_back(2)
    lax.fori_loop(8, 16, own_grads, 0, unroll=4)
    swap_own = swap(2 * turns, own.at[sib], own_rx)
    swap_own.start()
    store_q = pltpu.make_async_copy(dq_ref, dq_hbm, store_sem.at[CHUNKS])
    store_q.start()
    sent(0, out1, in1)
    sent(1, out2, mine)
    sent(2, out3, in3)
    told.wait_send()
    for turn in range(turns):
        swap_prev(turn).wait_send()
        swap_back(turn).wait_send()
    swap_own.wait()
    store_q.wait()

    def settle(c, _):
        own_rx[c] += own[core, c]
        return 0

    lax.fori_loop(0, cells, settle, 0, unroll=4)
    for turn in range(turns):
        lot(3, turn, out4, in4).wait_recv()

    def give(part):
        span = pl.ds(part * chunk, chunk)
        where = dkv_hbm.at[core, span]
        return (
            pltpu.make_async_copy(total_ref.at[span], where, store_sem.at[part]),
            swap(2 * turns + 1 + part, total_ref.at[span], where),
        )

    for part in range(CHUNKS):
        for i in range(chunk):
            c = part * chunk + i
            came = in4[pl.ds(jnp.maximum(slot[c], 0) * PARTS, PARTS)].astype(F32).reshape(cell, width)
            back_rows = jnp.where(row_at < PARTS, 0.0, came)
            for j in range(1, PARTS):
                back_rows = jnp.where(row_at == j * part_rows, came[j : j + 1, :], back_rows)
            total = own_rx[c] + jnp.where(slot[c] >= 0, back_rows, 0.0)
            total_ref[c] = total.astype(BF16)
        for copy in give(part):
            copy.start()

    sent(3, out4, in4)
    for part in range(CHUNKS):
        for copy in give(part):
            copy.wait()


def pin(x):
    return pltpu.with_memory_space_constraint(x, pltpu.HBM)


def on_device(n, query_heads, key_heads, value_heads, attend_grad, doc_ids, cell_plan):
    tokens, _, heads, width = query_heads.shape
    cells = cell_plan.shape[0]
    cell = tokens // cells
    crow = cell * heads

    n_slots = 3 * n // 4
    slots = pltpu.VMEM((n_slots * PARTS, cell // PARTS, width), BF16)
    both = pltpu.VMEM((2, n_slots * PARTS, cell // PARTS, width), BF16)
    hbm = pl.BlockSpec(memory_space=pl.ANY)
    wide = pltpu.VMEM((cells, crow, width), BF16)
    narrow = pltpu.VMEM((cells, cell, width), BF16)
    n_swaps = 2 * (n_slots * PARTS // n) + 1 + CHUNKS
    dq, dkv = pl.pallas_call(
        functools.partial(kernel, n, cells, cell, LONG, heads),
        out_shape=(
            jax.ShapeDtypeStruct((cells, crow, width), BF16),
            jax.ShapeDtypeStruct((2, cells, cell, width), BF16),
        ),
        in_specs=[hbm] * 6,
        out_specs=[hbm] * 2,
        scratch_shapes=[
            pltpu.SMEM((cells,), jnp.int32),
            pltpu.SMEM((tokens,), jnp.int32),
            pltpu.SMEM((n, 8), jnp.int32),
            pltpu.SMEM((n,), jnp.int32),
            pltpu.SMEM((cells,), jnp.int32),
            pltpu.SMEM((n_slots,), jnp.int32),
            pltpu.SMEM((cells,), jnp.int32),
            wide, narrow, narrow, wide, wide, narrow, narrow,
        ]
        + [slots] * 7
        + [
            both, both, slots,
            pltpu.VMEM((2, cells, cell, width), F32),
            pltpu.VMEM((cells, cell, width), F32),
            pltpu.VMEM((cells, 8, crow), F32),
            pltpu.VMEM((n_slots, 8, crow), F32),
            pltpu.VMEM((n_slots, cell, crow), BF16),
            pltpu.SemaphoreType.DMA((6,)),
            pltpu.SemaphoreType.DMA((2,)),
            pltpu.SemaphoreType.DMA((4, n_slots * PARTS // n)),
            pltpu.SemaphoreType.DMA((4, n_slots * PARTS // n)),
            pltpu.SemaphoreType.DMA((n_swaps,)),
            pltpu.SemaphoreType.DMA((n_swaps,)),
            pltpu.SemaphoreType.DMA((CHUNKS + 1,)),
        ],
        compiler_params=pltpu.CompilerParams(
            collective_id=0, has_side_effects=True, vmem_limit_bytes=48 * 2**20
        ),
    )(
        pin(cell_plan),
        pin(doc_ids),
        pin(query_heads.reshape(cells, crow, width)),
        pin(key_heads.reshape(cells, cell, width)),
        pin(value_heads.reshape(cells, cell, width)),
        pin(attend_grad.reshape(cells, crow, width)),
    )
    return (
        dq.reshape(tokens, 1, heads, width),
        dkv[0].reshape(tokens, 1, width),
        dkv[1].reshape(tokens, 1, width),
    )


def solution(mesh):
    wide = P("dp", "tensor", "section", None)
    narrow = P("dp", "tensor", None)
    return jax.shard_map(
        functools.partial(on_device, mesh.shape["dp"]),
        mesh=mesh,
        in_specs=(wide, narrow, narrow, wide, P("dp"), P("dp")),
        out_specs=(wide, narrow, narrow),
        check_vma=False,
    )
```

```python
import functools

import jax
import jax.numpy as jnp
from jax import lax
from jax.experimental import pallas as pl
from jax.experimental.pallas import tpu as pltpu
from jax.sharding import PartitionSpec as P

LONG = 8
CHUNKS = 4
PARTS = 4
RING = 8
MESH = pl.DeviceIdType.MESH
LOG2E = 1.4426950408889634
NEG = -1e30
F32 = jnp.float32
BF16 = jnp.bfloat16
NT = (((1,), (1,)), ((), ()))
TN = (((0,), (0,)), ((), ()))


def dot(a, b, dims=(((1,), (0,)), ((), ()))):
    return lax.dot_general(a, b, dims, preferred_element_type=F32)


def softmax_grads(keys, vals, quer, grad, mask, scale):
    scores = jnp.where(mask, dot(keys, quer, NT), NEG)
    prob_grad = dot(vals, grad, NT)
    top = jnp.max(scores, axis=0, keepdims=True)
    unnorm = jnp.exp2((scores - top) * (scale * LOG2E))
    probs = unnorm * (1.0 / jnp.sum(unnorm, axis=0, keepdims=True))
    delta = jnp.sum(probs * prob_grad, axis=0, keepdims=True)
    dscore = (probs * (prob_grad - delta)).astype(BF16)
    dv = dot(probs.astype(BF16), grad)
    dk = dot(dscore, quer) * scale
    dq = dot(dscore, keys, TN) * scale
    return dq, dk, dv


def kernel(
    n, cells, cell, long_cells, heads,
    plan_hbm, doc_hbm, q_hbm, k_hbm, v_hbm, g_hbm,
    dq_hbm, dkv_hbm,
    plan, doc, flags, rank, slot, inverse, bound, q_ref, k_ref, v_ref, g_ref, dq_ref, total_ref, marked,
    in1, out1, out2, in3, out3, in4, out4,
    prev, dprev, dprev_rx, own, own_rx, stats, final, dscores,
    load_sem, flag_sem, send_sem, recv_sem, sib_send, sib_recv, store_sem,
):
    me = lax.axis_index("dp")
    core = lax.axis_index("section")
    sib = 1 - core
    crow = cell * heads
    width = q_ref.shape[-1]
    scale = width ** -0.5
    chunk = cells // CHUNKS
    part_rows = cell // PARTS
    n_slots = 3 * n // 4
    turns = n_slots * PARTS // n
    per_turn = n_slots // turns
    ring = min(RING, n)
    lines = n // ring
    line_at, ring_at = me // ring, lax.rem(me, ring)

    def peer_of(k):
        turn = k // lines
        odd = lax.rem(turn, 2)
        offset = ring // 2 + odd * (turn + 1) // 2 - (1 - odd) * (turn // 2)
        line = lax.rem(line_at + lines - 1 - lax.rem(k, lines), lines)
        return line * ring + lax.rem(ring_at + offset, ring)

    def each_peer(act):
        def step(k, _):
            act(peer_of(k))
            return 0

        lax.fori_loop(0, n - 1, step, 0, unroll=True)

    barrier = pltpu.get_barrier_semaphore()

    def greet(peer):
        pl.semaphore_signal(barrier, inc=1, device_id={"dp": peer}, device_id_type=MESH)

    each_peer(greet)
    pl.semaphore_signal(barrier, inc=1, device_id={"section": sib}, device_id_type=MESH)

    loads = [
        pltpu.make_async_copy(src, dst, load_sem.at[i])
        for i, (src, dst) in enumerate(
            ((plan_hbm, plan), (doc_hbm, doc), (k_hbm, k_ref), (v_hbm, v_ref), (q_hbm, q_ref), (g_hbm, g_ref))
        )
    ]
    for load in loads:
        load.start()

    def launch(phase, turn, src, dst):
        def send(peer):
            pltpu.make_async_remote_copy(
                src_ref=src.at[turn * n + peer],
                dst_ref=dst.at[turn * n + me],
                send_sem=send_sem.at[phase, turn],
                recv_sem=recv_sem.at[phase, turn],
                device_id={"dp": peer},
                device_id_type=MESH,
            ).start()

        dst[turn * n + me] = src[turn * n + me]
        each_peer(send)

    def lot(phase, turn, src, dst):
        return pltpu.make_async_remote_copy(
            src_ref=src.at[pl.ds(0, n - 1)],
            dst_ref=dst.at[pl.ds(0, n - 1)],
            send_sem=send_sem.at[phase, turn],
            recv_sem=recv_sem.at[phase, turn],
            device_id={"section": sib},
            device_id_type=MESH,
        )

    def sent(phase, src, dst):
        for turn in range(turns):
            lot(phase, turn, src, dst).wait_send()

    def swap(which, src, dst):
        return pltpu.make_async_remote_copy(
            src_ref=src,
            dst_ref=dst,
            send_sem=sib_send.at[which],
            recv_sem=sib_recv.at[which],
            device_id={"section": sib},
            device_id_type=MESH,
        )

    loads[0].wait()
    for i in range(flags.shape[1]):
        flags[me, i] = plan[0]

    pl.semaphore_wait(barrier, n)

    def tell(peer):
        pltpu.make_async_remote_copy(
            src_ref=flags.at[me],
            dst_ref=flags.at[me],
            send_sem=flag_sem.at[0],
            recv_sem=flag_sem.at[1],
            device_id={"dp": peer},
            device_id_type=MESH,
        ).start()

    each_peer(tell)
    told = pltpu.make_async_remote_copy(
        src_ref=flags.at[pl.ds(0, n - 1)],
        dst_ref=flags.at[pl.ds(0, n - 1)],
        send_sem=flag_sem.at[0],
        recv_sem=flag_sem.at[1],
        device_id={"section": sib},
        device_id_type=MESH,
    )

    loads[1].wait()

    def bounds(c, _):
        base = c * cell
        lead = doc[base]
        last = jnp.int32(0)
        step = cell // 2
        while step:
            last = jnp.where(doc[base + last + step] == lead, last + step, last)
            step //= 2
        bound[c] = last + 1
        return 0

    lax.fori_loop(0, cells, bounds, 0, unroll=4)

    loads[2].wait()
    loads[3].wait()
    row_at = lax.broadcasted_iota(jnp.int32, (cell, width), 0)

    def mark(c, _):
        block = jnp.where(core == 0, k_ref[c], v_ref[c]).astype(F32)
        moved = block
        for i in range(1, PARTS):
            moved = jnp.where(row_at == i, block[i * part_rows : i * part_rows + 1, :], moved)
        moved = jnp.where(row_at % part_rows == 0, bound[c].astype(F32), moved)
        marked[c] = moved.astype(BF16)
        return 0

    lax.fori_loop(0, cells, mark, 0, unroll=4)

    loads[4].wait()
    loads[5].wait()
    long_len = long_cells * cell
    own[:, long_cells:] = jnp.zeros((2, cells - long_cells, cell, width), F32)
    dq_ref[long_cells:] = jnp.zeros((cells - long_cells, crow, width), BF16)
    long_key = lax.broadcasted_iota(jnp.int32, (long_len, crow), 0)
    long_query = lax.broadcasted_iota(jnp.int32, (long_len, crow), 1) // heads

    def long_step(c):
        seen = min(2 * (c // 2) + 2, long_cells)
        flat = (seen * cell, width)
        dq, dk, dv = softmax_grads(
            k_ref[:seen].reshape(flat), v_ref[:seen].reshape(flat), q_ref[c], g_ref[c],
            long_key[: seen * cell] <= long_query[: seen * cell] + c * cell, scale,
        )
        dq_ref[c] = dq.astype(BF16)
        for which, grads in ((0, dk), (1, dv)):
            grads = grads.reshape(seen, cell, width)
            if c == long_cells - 1:
                own[which, :seen] = grads
            else:
                own[which, :seen] += grads

    key_at = lax.broadcasted_iota(jnp.int32, (cell, crow), 0)
    query_at = lax.broadcasted_iota(jnp.int32, (cell, crow), 1) // heads
    causal = key_at <= query_at
    query_row = query_at[0:1, :]
    moved_at = jnp.where(key_at < PARTS, key_at * part_rows, key_at)
    moved_at = jnp.where(key_at % part_rows == 0, -1, moved_at)

    def own_block(c):
        low = jnp.where(query_row < bound[c], 0, bound[c])
        scores = jnp.where(causal & (key_at >= low), dot(k_ref[c], q_ref[c], NT), NEG)
        return scores, dot(v_ref[c], g_ref[c], NT)

    def own_stats(c, _):
        scores, prob_grad = own_block(c)
        top = jnp.max(scores, axis=0, keepdims=True)
        unnorm = jnp.exp2((scores - top) * (scale * LOG2E))
        stats[c, 0:1] = top
        stats[c, 1:2] = jnp.sum(unnorm, axis=0, keepdims=True)
        stats[c, 2:3] = jnp.sum(unnorm * prob_grad, axis=0, keepdims=True)
        return 0

    lax.fori_loop(0, cells, own_stats, 0, unroll=4)

    for c in range(long_cells - 1, long_cells - 2, -1):
        long_step(c)
    told.wait_recv()

    keepers = jnp.int32(0)
    for d in range(n):
        rank[d] = d - keepers
        keepers += jnp.where(flags[d, 0] < 0, 1, 0)
    for c in range(cells):
        slot[c] = jnp.where(plan[c] >= 0, rank[jnp.maximum(plan[c], 0)], -1)

    def fill(j, _):
        at = jnp.int32(-1)
        for c in range(cells):
            at = jnp.where(slot[c] == j, c, at)
        inverse[j] = at
        block = jnp.where(at >= 0, marked[jnp.maximum(at, 0)], jnp.zeros((cell, width), BF16))
        out1[pl.ds(j * PARTS, PARTS)] = block.reshape(PARTS, part_rows, width)
        return 0


    for turn in range(turns):
        lax.fori_loop(turn * per_turn, (turn + 1) * per_turn, fill, 0, unroll=2)
        launch(0, turn, out1, in1)
    for c in range(long_cells - 2, -1, -1):
        long_step(c)

    def hub(turn):
        def step(r, last):
            at = turn * n + r
            out2[at] = last.astype(BF16)
            block = in1[at].astype(F32)
            return jnp.where(block[0:1, :] > 0.0, block, last)

        lax.fori_loop(0, n, step, jnp.zeros((part_rows, width), F32), unroll=8)

    mine = prev.at[core]
    for turn in range(turns):
        lot(0, turn, out1, in1).wait_recv()
        hub(turn)
        launch(1, turn, out2, mine)

    def swap_prev(turn):
        span = pl.ds(turn * n, n)
        return swap(turn, prev.at[core, span], prev.at[core, span])

    def slot_rows(j):
        return pl.ds(j * PARTS, PARTS)

    def cross(j):
        c = jnp.maximum(inverse[j], 0)
        quer, grad = q_ref[c], g_ref[c]
        prev_key = prev[0, slot_rows(j)].reshape(cell, width)
        mark = prev_key.astype(F32)[0:1, :]
        mark = jnp.concatenate([mark] * (crow // width), axis=1)
        mark = jnp.where(mark > 0.0, mark.astype(jnp.int32), cell)
        low = jnp.where(query_row < bound[c], mark, cell)
        scores = jnp.where(moved_at >= low, dot(prev_key, quer, NT), NEG)
        prob_grad = dot(prev[1, slot_rows(j)].reshape(cell, width), grad, NT)
        own_top = stats[c, 0:1]
        top = jnp.maximum(jnp.max(scores, axis=0, keepdims=True), own_top)
        unnorm = jnp.exp2((scores - top) * (scale * LOG2E))
        shrink = jnp.exp2((own_top - top) * (scale * LOG2E))
        inv = 1.0 / (jnp.sum(unnorm, axis=0, keepdims=True) + shrink * stats[c, 1:2])
        delta = inv * (
            jnp.sum(unnorm * prob_grad, axis=0, keepdims=True) + shrink * stats[c, 2:3]
        )
        probs = unnorm * inv
        dscore = (probs * (prob_grad - delta)).astype(BF16)
        final[j, 0:1] = top
        final[j, 1:2] = inv
        final[j, 2:3] = delta
        dscores[j] = dscore
        shape = (PARTS, part_rows, width)
        dprev[0, slot_rows(j)] = (dot(dscore, quer) * scale).astype(BF16).reshape(shape)
        dprev[1, slot_rows(j)] = dot(probs.astype(BF16), grad).astype(BF16).reshape(shape)

    def swap_back(turn):
        span = pl.ds(turn * n, n)
        return swap(turns + turn, dprev.at[sib, span], dprev_rx.at[span])

    def attend(turn):
        swap_prev(turn).wait_recv()
        for j in range(turn * per_turn, (turn + 1) * per_turn):
            cross(j)
        swap_back(turn).start()

    def give_back(turn):
        swap_back(turn).wait_recv()
        span = pl.ds(turn * n, n)
        out3[span] = (dprev[core, span].astype(F32) + dprev_rx[span].astype(F32)).astype(BF16)
        launch(2, turn, out3, in3)

    def own_grads(c, _):
        j = jnp.maximum(slot[c], 0)
        quer, grad = q_ref[c], g_ref[c]
        scores, prob_grad = own_block(c)
        probs = jnp.exp2((scores - final[j, 0:1]) * (scale * LOG2E)) * final[j, 1:2]
        dscore = (probs * (prob_grad - final[j, 2:3])).astype(BF16)
        dv = dot(probs.astype(BF16), grad)
        dk = dot(dscore, quer) * scale
        both = jnp.concatenate([dscores[j], dscore], axis=0)
        keys = jnp.concatenate([prev[0, slot_rows(j)].reshape(cell, width), k_ref[c]], axis=0)
        dq = dot(both, keys, TN) * scale
        kept = plan[c] < 0
        dq_ref[c] = jnp.where(kept, dq_ref[c].astype(F32), dq).astype(BF16)
        own[0, c] = jnp.where(kept, own[0, c], dk)
        own[1, c] = jnp.where(kept, own[1, c], dv)
        return 0

    def hub_back(turn):
        def step(k, later):
            at = turn * n + n - 1 - k
            out4[at] = later.astype(BF16)
            marks = in1[at].astype(F32)
            return jnp.where(marks[0:1, :] > 0.0, in3[at].astype(F32), later)

        lax.fori_loop(0, n, step, jnp.zeros((part_rows, width), F32), unroll=8)

    def pass_back(turn):
        lot(2, turn, out3, in3).wait_recv()
        hub_back(turn)
        launch(3, turn, out4, in4)

    def arrive(turn):
        lot(1, turn, out2, mine).wait_recv()
        swap_prev(turn).start()

    arrive(0)
    attend(0)
    arrive(1)
    give_back(0)
    attend(1)
    arrive(2)
    give_back(1)
    attend(2)
    give_back(2)
    pass_back(0)
    lax.fori_loop(0, 4, own_grads, 0, unroll=4)
    pass_back(1)
    lax.fori_loop(4, 8, own_grads, 0, unroll=4)
    pass_back(2)
    lax.fori_loop(8, 16, own_grads, 0, unroll=4)
    swap_own = swap(2 * turns, own.at[sib], own_rx)
    swap_own.start()
    store_q = pltpu.make_async_copy(dq_ref, dq_hbm, store_sem.at[CHUNKS])
    store_q.start()
    sent(0, out1, in1)
    sent(1, out2, mine)
    sent(2, out3, in3)
    told.wait_send()
    for turn in range(turns):
        swap_prev(turn).wait_send()
        swap_back(turn).wait_send()
    swap_own.wait()
    store_q.wait()

    def settle(c, _):
        own_rx[c] += own[core, c]
        return 0

    lax.fori_loop(0, cells, settle, 0, unroll=4)
    for turn in range(turns):
        lot(3, turn, out4, in4).wait_recv()

    def give(part):
        span = pl.ds(part * chunk, chunk)
        where = dkv_hbm.at[core, span]
        return (
            pltpu.make_async_copy(total_ref.at[span], where, store_sem.at[part]),
            swap(2 * turns + 1 + part, total_ref.at[span], where),
        )

    for part in range(CHUNKS):
        for i in range(chunk):
            c = part * chunk + i
            came = in4[pl.ds(jnp.maximum(slot[c], 0) * PARTS, PARTS)].astype(F32).reshape(cell, width)
            back_rows = jnp.where(row_at < PARTS, 0.0, came)
            for j in range(1, PARTS):
                back_rows = jnp.where(row_at == j * part_rows, came[j : j + 1, :], back_rows)
            total = own_rx[c] + jnp.where(slot[c] >= 0, back_rows, 0.0)
            total_ref[c] = total.astype(BF16)
        for copy in give(part):
            copy.start()

    sent(3, out4, in4)
    for part in range(CHUNKS):
        for copy in give(part):
            copy.wait()


def pin(x):
    return pltpu.with_memory_space_constraint(x, pltpu.HBM)


def on_device(n, query_heads, key_heads, value_heads, attend_grad, doc_ids, cell_plan):
    tokens, _, heads, width = query_heads.shape
    cells = cell_plan.shape[0]
    cell = tokens // cells
    crow = cell * heads

    n_slots = 3 * n // 4
    slots = pltpu.VMEM((n_slots * PARTS, cell // PARTS, width), BF16)
    both = pltpu.VMEM((2, n_slots * PARTS, cell // PARTS, width), BF16)
    hbm = pl.BlockSpec(memory_space=pl.ANY)
    wide = pltpu.VMEM((cells, crow, width), BF16)
    narrow = pltpu.VMEM((cells, cell, width), BF16)
    n_swaps = 2 * (n_slots * PARTS // n) + 1 + CHUNKS
    dq, dkv = pl.pallas_call(
        functools.partial(kernel, n, cells, cell, LONG, heads),
        out_shape=(
            jax.ShapeDtypeStruct((cells, crow, width), BF16),
            jax.ShapeDtypeStruct((2, cells, cell, width), BF16),
        ),
        in_specs=[hbm] * 6,
        out_specs=[hbm] * 2,
        scratch_shapes=[
            pltpu.SMEM((cells,), jnp.int32),
            pltpu.SMEM((tokens,), jnp.int32),
            pltpu.SMEM((n, 8), jnp.int32),
            pltpu.SMEM((n,), jnp.int32),
            pltpu.SMEM((cells,), jnp.int32),
            pltpu.SMEM((n_slots,), jnp.int32),
            pltpu.SMEM((cells,), jnp.int32),
            wide, narrow, narrow, wide, wide, narrow, narrow,
        ]
        + [slots] * 7
        + [
            both, both, slots,
            pltpu.VMEM((2, cells, cell, width), F32),
            pltpu.VMEM((cells, cell, width), F32),
            pltpu.VMEM((cells, 8, crow), F32),
            pltpu.VMEM((n_slots, 8, crow), F32),
            pltpu.VMEM((n_slots, cell, crow), BF16),
            pltpu.SemaphoreType.DMA((6,)),
            pltpu.SemaphoreType.DMA((2,)),
            pltpu.SemaphoreType.DMA((4, n_slots * PARTS // n)),
            pltpu.SemaphoreType.DMA((4, n_slots * PARTS // n)),
            pltpu.SemaphoreType.DMA((n_swaps,)),
            pltpu.SemaphoreType.DMA((n_swaps,)),
            pltpu.SemaphoreType.DMA((CHUNKS + 1,)),
        ],
        compiler_params=pltpu.CompilerParams(
            collective_id=0, has_side_effects=True, vmem_limit_bytes=48 * 2**20
        ),
    )(
        pin(cell_plan),
        pin(doc_ids),
        pin(query_heads.reshape(cells, crow, width)),
        pin(key_heads.reshape(cells, cell, width)),
        pin(value_heads.reshape(cells, cell, width)),
        pin(attend_grad.reshape(cells, crow, width)),
    )
    return (
        dq.reshape(tokens, 1, heads, width),
        dkv[0].reshape(tokens, 1, width),
        dkv[1].reshape(tokens, 1, width),
    )


def solution(mesh):
    wide = P("dp", "tensor", "section", None)
    narrow = P("dp", "tensor", None)
    return jax.shard_map(
        functools.partial(on_device, mesh.shape["dp"]),
        mesh=mesh,
        in_specs=(wide, narrow, narrow, wide, P("dp"), P("dp")),
        out_specs=(wide, narrow, narrow),
        check_vma=False,
    )
```
